32 devices in a mesh: section: 4 (over y, x), expert: 8 (over z, core).
Axes of the slice: x: 2, y: 2, z: 4, core: 2. Of those that a mesh axis runs over, the one named last changes fastest.
Arguments:
- upstream: bfloat16 [4, 1024, 3584], P('section', 'expert'), may hold values from -0.59765625 to 0.59765625
- routes: int32 [4, 1024, 2], P('section', 'expert'), may hold values from 0 to 7, all different within a row; in each aligned block of 128 rows (0 to 127, 128 to 255, ..., all dimensions but the last counted through in order) at most 48 rows name the same one
- gates: float32 [4, 1024, 2], P('section', 'expert'), may hold values from 0.1 to 1
- w_gate: bfloat16 [4, 3584, 8192], P('section', None, 'expert'), may hold values from -0.09375 to 0.09375
- w_up: bfloat16 [4, 3584, 8192], P('section', None, 'expert'), may hold values from -0.09375 to 0.09375
- w_down: bfloat16 [4, 8192, 3584], P('section', 'expert'), may hold values from -0.1875 to 0.1875
- stash_q: bfloat16 [4, 3072, 3584], P('section', 'expert'), may hold values from -448 to 448
- stash_scale: float32 [4, 3072, 28], P('section', 'expert'), may hold values from 0.004 to 0.04
Outputs:
- grad_input: bfloat16 [4, 1024, 3584], P('section', 'expert')
- grad_gates: float32 [4, 1024, 2], P('section', 'expert')
- grad_w_gate: bfloat16 [4, 3584, 8192], P('section', None, 'expert')
- grad_w_up: bfloat16 [4, 3584, 8192], P('section', None, 'expert')
- grad_w_down: bfloat16 [4, 8192, 3584], P('section', 'expert')
The draws below stay inside these ranges and needn't reach their ends.
Inputs may be any that keep to these rules, and one draw needn't show every extreme that they name: `routes`: in each section, each token names 2 different experts, and within the 128 tokens of one device no expert is named more than 48 times; some expert is named exactly 48 times.
All inputs are finite; a program needn't handle non-finite values.
Results may differ from the reference program's by a relative error of at most 0.014.
Values may be sent and summed in bfloat16 or wider, within the bound.
No kernel may reach another device: no remote copies, remote signals or barrier semaphores. Data moves between devices by JAX's collectives and lax.ppermute only.
A program may use at most 256 MiB of HBM per device.

```python
import math
import jax
import jax.numpy as jnp
import numpy as np
from jax import lax

D = 3584
FF = 1024
EXPERTS = 8
TOPK = 2
TOK_DEV = 128
CAP = 48
SLOTS = 384
TOKENS = 1024
SECTIONS = 4
N_SECTION = 4
N_EXPERT = 8


def level_of(key, shape, pieces, smallest, largest):
    factor_of, own = 1.0, jax.random.fold_in(key, 6)
    for dim, blocks in pieces:
        draws = jnp.exp(jax.random.uniform(jax.random.fold_in(own, dim), (blocks,), jnp.float32, smallest / len(pieces), largest / len(pieces)))
        factor_of = factor_of * jnp.repeat(draws, shape[dim] // blocks).reshape([-1 if axis == dim else 1 for axis in range(len(shape))])
    return factor_of


def shared_out(own_key, own, number, rows, amount, top, limit, skew):
    order = jax.random.permutation(own_key, amount)
    heavy_load, common = shares(amount, rows * top, limit, skew, True), shares(amount, rows * top, limit, skew, False)
    places = jnp.arange(amount)

    def named(sizes, offset_by):
        used = int((sizes > 0).sum())
        fixed = max(1, used // 4)
        shifted = fixed + (places - fixed + offset_by * (used - fixed)) % max(1, amount - fixed)
        return jnp.zeros((amount,), jnp.int32).at[order[jnp.where(places < fixed, places, shifted)]].set(jnp.asarray(sizes, jnp.int32))

    sizes = jnp.where(number % 4 == 0, named(heavy_load, number // 4), named(common, number - number // 4 - 1))
    mixed = jax.random.permutation(jax.random.fold_in(own, 3), amount)
    donor, taker = mixed[0:amount // 2 * 2:2], mixed[1:amount // 2 * 2:2]
    slack = jnp.minimum(sizes[donor] - 1, limit - sizes[taker]) // 2
    slack = jnp.where((donor == order[0]) | (taker == order[0]) | (sizes[taker] == 0), 0, jnp.maximum(slack, 0))
    shifted = jax.random.randint(jax.random.fold_in(own, 4), (amount // 2,), 0, 1 << 20) % (slack + 1)
    sizes = sizes.at[donor].add(-shifted).at[taker].add(shifted)
    labels = jnp.searchsorted(jnp.cumsum(sizes), jnp.arange(rows * top), side="right").astype(jnp.int32)
    listing = labels.reshape(top, rows).T
    listing = listing[jax.random.permutation(jax.random.fold_in(own, 1), rows)]
    offset_by = jax.random.randint(jax.random.fold_in(own, 2), (rows, 1), 0, top)
    return jnp.take_along_axis(listing, (jnp.arange(top)[None, :] + offset_by) % top, axis=1)


def shares(count, total, limit, slope, full):
    portions = [(1 << 20) // math.isqrt(standing ** slope) + 1 for standing in range(1, count + 1)]
    largest = limit if full else min(limit, max(-(-total // count), total * portions[0] // sum(portions)))
    least = 1 if total - largest >= count - 1 else 0
    holding, rest = [largest] + [least] * (count - 1), total - largest - least * (count - 1)
    while rest > 0:
        movable = [i for i in range(1, count) if holding[i] < largest] or [i for i in range(1, count) if holding[i] < limit]
        pool, left = sum([portions[i] for i in movable]), rest
        for i in movable:
            addition = min(limit - holding[i], max(1, left * portions[i] // pool), rest)
            holding[i] = holding[i] + addition
            rest = rest - addition
    return np.array(holding)


def centred(own_key, extent, spread, limit, pieces=(), kind=jnp.bfloat16):
    values = spread * jax.random.normal(own_key, extent, jnp.float32)
    if pieces:
        values = values * level_of(own_key, extent, pieces, -0.22, 0.18)
    return jnp.clip(values, -limit, limit).astype(kind)


def setup_inputs(seed: int = 0) -> dict:
    key_list = jax.random.split(jax.random.key(seed), 9)
    upstream = centred(key_list[0], (SECTIONS, TOKENS, D), 0.1, 0.59765625, ((0, 4), (1, 8)))
    routes_keys = jax.random.split(jax.random.fold_in(key_list[1], 1), SECTIONS * TOKENS // TOK_DEV)
    routes_turns = jax.random.permutation(jax.random.fold_in(key_list[1], 3), SECTIONS * TOKENS // TOK_DEV)
    routes = jax.vmap(lambda own, number: shared_out(jax.random.fold_in(key_list[1], 2), own, number, TOK_DEV, EXPERTS, TOPK, CAP, 2))(routes_keys, routes_turns).reshape((SECTIONS, TOKENS, TOPK))
    gates = jnp.clip(jnp.exp(math.log(1.0) - 2.3025851 * jax.random.uniform(key_list[2], (SECTIONS, TOKENS, TOPK), jnp.float32) ** level_of(key_list[2], (SECTIONS, TOKENS, TOPK), ((0, 4), (1, 8)), -0.2, 0.2)), 0.1, 1.0)
    w_gate = centred(key_list[3], (SECTIONS, D, EXPERTS * FF), D ** -0.5, 0.09375, ((0, 4), (2, 8)))
    w_up = centred(key_list[4], (SECTIONS, D, EXPERTS * FF), D ** -0.5, 0.09375, ((0, 4), (2, 8)))
    w_down = centred(key_list[5], (SECTIONS, EXPERTS * FF, D), FF ** -0.5, 0.1875, ((0, 4), (1, 8)))
    stash_q = centred(key_list[6], (SECTIONS, N_EXPERT * SLOTS, D), 64.0, 448.0, ((0, 4), (1, 8)))
    stash_scale = jnp.clip(jnp.exp(math.log(0.04) - 2.30258502 * jax.random.uniform(key_list[7], (SECTIONS, N_EXPERT * SLOTS, D // 128), jnp.float32) ** level_of(key_list[7], (SECTIONS, N_EXPERT * SLOTS, D // 128), ((0, 4), (1, 8)), -0.2, 0.2)), 0.004, 0.04)
    return {"upstream": upstream, "routes": routes, "gates": gates, "w_gate": w_gate, "w_up": w_up, "w_down": w_down, "stash_q": stash_q, "stash_scale": stash_scale}


def slot_work(codes, scales, cotangent, weights, gate_cols, up_cols, down_rows):
    count, width = codes.shape
    blocks = width // 128
    inputs = (codes.astype(jnp.float32).reshape(count, blocks, 128) * scales[:, :, None]).reshape(count, width).astype(jnp.bfloat16)
    gate_pre = jnp.dot(inputs, gate_cols, preferred_element_type=jnp.float32)
    up_pre = jnp.dot(inputs, up_cols, preferred_element_type=jnp.float32)
    sigma = jax.nn.sigmoid(gate_pre)
    swish = gate_pre * sigma
    hidden = swish * up_pre
    scaled_hidden = (weights[:, None] * hidden).astype(jnp.bfloat16)
    grad_down = lax.dot_general(scaled_hidden, cotangent, (((0,), (0,)), ((), ())), preferred_element_type=jnp.float32)
    raw_grad = lax.dot_general(cotangent, down_rows, (((1,), (1,)), ((), ())), preferred_element_type=jnp.float32)
    gate_part = jnp.sum(hidden * raw_grad, axis=1)
    grad_hidden = weights[:, None] * raw_grad
    grad_gate_pre = (grad_hidden * up_pre * sigma * (1.0 + gate_pre * (1.0 - sigma))).astype(jnp.bfloat16)
    grad_up_pre = (grad_hidden * swish).astype(jnp.bfloat16)
    grad_gate_w = lax.dot_general(inputs, grad_gate_pre, (((0,), (0,)), ((), ())), preferred_element_type=jnp.float32)
    grad_up_w = lax.dot_general(inputs, grad_up_pre, (((0,), (0,)), ((), ())), preferred_element_type=jnp.float32)
    input_sum = lax.dot_general(grad_gate_pre, gate_cols, (((1,), (1,)), ((), ())), preferred_element_type=jnp.float32)
    input_sum = input_sum + lax.dot_general(grad_up_pre, up_cols, (((1,), (1,)), ((), ())), preferred_element_type=jnp.float32)
    return grad_gate_w, grad_up_w, grad_down, input_sum.astype(jnp.bfloat16), gate_part


def section_pass(cotangent, routing, gate_vals, gate_w, up_w, down_w, codes, scales):
    hsplit = N_EXPERT // EXPERTS
    ff_dev = FF // hsplit
    slots = CAP * N_EXPERT
    pairs = TOK_DEV * TOPK
    flat = routing.reshape(N_EXPERT, pairs).astype(jnp.int32)
    onehot = (flat[:, :, None] == jnp.arange(EXPERTS, dtype=jnp.int32)[None, None, :]).astype(jnp.int32)
    before = jnp.cumsum(onehot, axis=1) - onehot
    slot = jnp.sum(before * onehot, axis=2).astype(jnp.int32)
    source = jnp.arange(N_EXPERT, dtype=jnp.int32)[:, None]
    target = ((flat * N_EXPERT + source) * CAP + slot).reshape(-1).astype(jnp.int32)
    token = (jnp.arange(pairs, dtype=jnp.int32)[None, :] // TOPK + source * TOK_DEV).reshape(-1).astype(jnp.int32)
    row_buf = jnp.zeros((EXPERTS * slots, D), jnp.bfloat16).at[target].set(cotangent[token])
    weight_buf = jnp.zeros((EXPERTS * slots,), jnp.float32).at[target].set(gate_vals.reshape(-1))
    row_buf = row_buf.reshape(EXPERTS, slots, D)
    weight_buf = weight_buf.reshape(EXPERTS, slots)

    def device(index):
        expert = index // hsplit
        rows = lax.dynamic_index_in_dim(row_buf, expert, 0, keepdims=False)
        weights = lax.dynamic_index_in_dim(weight_buf, expert, 0, keepdims=False)
        gate_cols = lax.dynamic_slice_in_dim(gate_w, index * ff_dev, ff_dev, 1)
        up_cols = lax.dynamic_slice_in_dim(up_w, index * ff_dev, ff_dev, 1)
        down_rows = lax.dynamic_slice_in_dim(down_w, index * ff_dev, ff_dev, 0)
        code_rows = lax.dynamic_slice_in_dim(codes, index * slots, slots, 0)
        scale_rows = lax.dynamic_slice_in_dim(scales, index * slots, slots, 0)
        return slot_work(code_rows, scale_rows, rows, weights, gate_cols, up_cols, down_rows)

    grad_gw, grad_uw, grad_dw, input_part, gate_part = lax.map(device, jnp.arange(N_EXPERT, dtype=jnp.int32))
    summed = jnp.sum(input_part.reshape(EXPERTS, hsplit, slots, D).astype(jnp.float32), axis=1).reshape(EXPERTS * slots, D)
    gate_sum = jnp.sum(gate_part.reshape(EXPERTS, hsplit, slots), axis=1).reshape(EXPERTS * slots)
    grad_input = jnp.sum(summed[target].reshape(N_EXPERT * TOK_DEV, TOPK, D), axis=1).astype(jnp.bfloat16)
    grad_gates = gate_sum[target].reshape(N_EXPERT * TOK_DEV, TOPK)
    grad_gw = jnp.transpose(grad_gw, (1, 0, 2)).reshape(D, N_EXPERT * ff_dev).astype(jnp.bfloat16)
    grad_uw = jnp.transpose(grad_uw, (1, 0, 2)).reshape(D, N_EXPERT * ff_dev).astype(jnp.bfloat16)
    grad_dw = grad_dw.reshape(N_EXPERT * ff_dev, D).astype(jnp.bfloat16)
    return grad_input, grad_gates, grad_gw, grad_uw, grad_dw


def reference(upstream, routes, gates, w_gate, w_up, w_down, stash_q, stash_scale):
    results = []
    for section_index in range(N_SECTION):
        nxt = (section_index + 1) % N_SECTION
        results.append(section_pass(upstream[nxt], routes[section_index], gates[section_index], w_gate[section_index], w_up[section_index], w_down[section_index], stash_q[section_index], stash_scale[section_index]))
    return (jnp.stack([item[0] for item in results]), jnp.stack([item[1] for item in results]), jnp.stack([item[2] for item in results]), jnp.stack([item[3] for item in results]), jnp.stack([item[4] for item in results]))
```

```python
import jax
import jax.numpy as jnp
from jax import lax
from jax.sharding import PartitionSpec as P

EXPERTS = 8
CAP = 48
CHUNKS = 4


def shifted(x, axis, by):
    size = lax.axis_size(axis)
    return lax.ppermute(x, axis, [(i, (i + by) % size) for i in range(size)])


def slot_work(codes, scales, cotangent, weights, gate_cols, up_cols, down_rows):
    count, width = codes.shape
    blocks = width // 128
    inputs = (
        (codes.astype(jnp.float32).reshape(count, blocks, 128) * scales[:, :, None])
        .reshape(count, width)
        .astype(jnp.bfloat16)
    )
    gate_pre = jnp.dot(inputs, gate_cols, preferred_element_type=jnp.float32)
    up_pre = jnp.dot(inputs, up_cols, preferred_element_type=jnp.float32)
    sigma = jax.nn.sigmoid(gate_pre)
    swish = gate_pre * sigma
    hidden = swish * up_pre
    scaled_hidden = (weights[:, None] * hidden).astype(jnp.bfloat16)
    grad_down = lax.dot_general(
        scaled_hidden, cotangent, (((0,), (0,)), ((), ())), preferred_element_type=jnp.float32
    )
    raw_grad = lax.dot_general(
        cotangent, down_rows, (((1,), (1,)), ((), ())), preferred_element_type=jnp.float32
    )
    gate_part = jnp.sum(hidden * raw_grad, axis=1)
    grad_hidden = weights[:, None] * raw_grad
    grad_gate_pre = (grad_hidden * up_pre * sigma * (1.0 + gate_pre * (1.0 - sigma))).astype(
        jnp.bfloat16
    )
    grad_up_pre = (grad_hidden * swish).astype(jnp.bfloat16)
    grad_gate_w = lax.dot_general(
        inputs, grad_gate_pre, (((0,), (0,)), ((), ())), preferred_element_type=jnp.float32
    )
    grad_up_w = lax.dot_general(
        inputs, grad_up_pre, (((0,), (0,)), ((), ())), preferred_element_type=jnp.float32
    )
    input_sum = lax.dot_general(
        grad_gate_pre, gate_cols, (((1,), (1,)), ((), ())), preferred_element_type=jnp.float32
    )
    input_sum = input_sum + lax.dot_general(
        grad_up_pre, up_cols, (((1,), (1,)), ((), ())), preferred_element_type=jnp.float32
    )
    return (grad_gate_w, grad_up_w, grad_down, input_sum.astype(jnp.bfloat16), gate_part)


def general(upstream, routes, gates, w_gate, w_up, w_down, stash_q, stash_scale):
    cotangent = shifted(upstream[0], "section", -1)
    tok_dev = routes.shape[1]
    topk = routes.shape[2]
    width = cotangent.shape[1]
    groups = lax.axis_size("expert")
    hsplit = groups // EXPERTS
    slots = groups * CAP
    flat = routes[0].reshape(-1)
    onehot = (flat[:, None] == jnp.arange(EXPERTS, dtype=jnp.int32)[None, :]).astype(jnp.int32)
    before = jnp.cumsum(onehot, axis=0) - onehot
    slot = jnp.sum(before * onehot, axis=1)
    target = flat * CAP + slot
    token = jnp.arange(tok_dev * topk, dtype=jnp.int32) // topk
    row_buf = jnp.zeros((EXPERTS * CAP, width), jnp.bfloat16).at[target].set(cotangent[token])
    weight_buf = jnp.zeros((EXPERTS * CAP,), jnp.float32).at[target].set(gates[0].reshape(-1))
    send_rows = jnp.repeat(row_buf.reshape(EXPERTS, CAP, width), hsplit, axis=0)
    send_weights = jnp.repeat(weight_buf.reshape(EXPERTS, CAP), hsplit, axis=0)
    got_rows, got_weights = (
        lax.all_to_all(send_rows, "expert", split_axis=0, concat_axis=0, tiled=True),
        lax.all_to_all(
            send_weights.astype(jnp.bfloat16), "expert", split_axis=0, concat_axis=0, tiled=True
        ).astype(send_weights.dtype),
    )
    rows = got_rows.reshape(slots, width)
    weights = got_weights.reshape(slots)
    grad_gw, grad_uw, grad_dw, input_part, gate_part = slot_work(
        stash_q[0], stash_scale[0], rows, weights, w_gate[0], w_up[0], w_down[0]
    )
    back_rows, back_gates = (
        lax.all_to_all(
            input_part.reshape(groups, CAP, width), "expert", split_axis=0, concat_axis=0, tiled=True
        ),
        lax.all_to_all(
            gate_part.reshape(groups, CAP).astype(jnp.bfloat16),
            "expert",
            split_axis=0,
            concat_axis=0,
            tiled=True,
        ).astype(jnp.float32),
    )
    summed = jnp.sum(
        back_rows.reshape(EXPERTS, hsplit, CAP, width).astype(jnp.float32), axis=1
    ).reshape(EXPERTS * CAP, width)
    gate_sum = jnp.sum(
        back_gates.reshape(EXPERTS, hsplit, CAP).astype(jnp.float32), axis=1
    ).reshape(EXPERTS * CAP)
    grad_input = jnp.sum(summed[target].reshape(tok_dev, topk, width), axis=1).astype(jnp.bfloat16)
    grad_gates = gate_sum[target].reshape(tok_dev, topk)
    return (
        grad_input[None],
        grad_gates[None],
        grad_gw.astype(jnp.bfloat16)[None],
        grad_uw.astype(jnp.bfloat16)[None],
        grad_dw.astype(jnp.bfloat16)[None],
    )


def chip_pairs(moves):
    return [(2 * a + core, 2 * b + core) for a, b in moves for core in range(2)]


INNER_SWAP = chip_pairs([(1, 2), (2, 1)])
END_TO_FAR = chip_pairs([(0, 2), (3, 1)])
FAR_TO_END = chip_pairs([(2, 0), (1, 3)])
HALF_SWAP = chip_pairs([(0, 1), (1, 0), (2, 3), (3, 2)])
INNER_TO_END = chip_pairs([(1, 0), (2, 3)])
END_TO_INNER = chip_pairs([(0, 1), (3, 2)])
CORE_SWAP = [(i, i ^ 1) for i in range(8)]


def send(x, pairs):
    return lax.ppermute(x, "expert", pairs)


def gathered(x):
    me = lax.axis_index("expert")
    x = x[None]
    for bit in (1, 2, 4):
        other = send(x, [(i, i ^ bit) for i in range(8)])
        mine_first = (me & bit) == 0
        x = jnp.concatenate(
            [jnp.where(mine_first, x, other), jnp.where(mine_first, other, x)], axis=0
        )
    return x


def mm(a, b, dims):
    return lax.dot_general(a, b, (dims, ((), ())), preferred_element_type=jnp.float32)


def relayed(upstream, routes, gates, w_gate, w_up, w_down, stash_q, stash_scale):
    bf16, f32 = jnp.bfloat16, jnp.float32
    tokens, width = upstream.shape[1], upstream.shape[2]
    blocks = width // 128
    cuts = [128 * (blocks * j // CHUNKS) for j in range(CHUNKS + 1)]
    spans = list(zip(cuts[:-1], cuts[1:]))
    me = lax.axis_index("expert")
    chip, core = me // 2, me % 2
    mate = chip ^ 1
    far_inner = jnp.where(chip >= 2, 1, 2)
    far_end = jnp.where(chip >= 2, 0, 3)

    route = routes[0].T
    ids = jnp.arange(EXPERTS, dtype=jnp.int32)[None, :, None]
    hit = route[:, None, :] == ids
    named = jnp.any(hit, axis=0)
    earlier = (jnp.arange(tokens)[:, None] < jnp.arange(tokens)[None, :]).astype(bf16)
    count = mm(named.astype(bf16), earlier, ((1,), (0,)))
    plan = jnp.where(named, count, -1.0)
    gate_of = jnp.sum(jnp.where(hit, gates[0].T[:, None, :], 0.0), axis=0)

    everyone = gathered(jnp.concatenate([plan, gate_of], axis=0))
    plans = everyone[:, :EXPERTS].reshape(8 * EXPERTS, tokens)
    gates_all = everyone[:, EXPERTS:].reshape(8 * EXPERTS, tokens)

    def picked(table, index):
        choose = (index[:, None] == jnp.arange(table.shape[0])[None, :]).astype(f32)
        return jnp.sum(choose[:, :, None] * table[None], axis=1)

    slot_ids = jnp.arange(CAP, dtype=f32)[None, :, None]

    def selection(rows):
        return (rows[:, None, :] == slot_ids).astype(bf16).reshape(-1, tokens)

    def pair(at):
        return [2 * at + core, 2 * at + 1 - core]

    own_sel = selection(picked(plan, jnp.stack(pair(chip) + pair(mate))))
    to_here, to_mate = own_sel[: 2 * CAP], own_sel[2 * CAP :]
    sources = [2 * far_inner + core, 2 * far_end + core]
    index = jnp.stack([s * EXPERTS + f for s in sources for f in pair(chip) + pair(mate)])
    far_sel = selection(picked(plans, index)).reshape(2, 2, 2 * CAP, tokens)

    order = jnp.stack(
        [2 * at + k for k in (core, 1 - core) for at in (chip, mate, far_inner, far_end)]
    )
    mine = order * EXPERTS + me
    weights = jnp.sum(
        jnp.where(
            picked(plans, mine)[:, None, :] == slot_ids, picked(gates_all, mine)[:, None, :], 0.0
        ),
        axis=2,
    ).reshape(-1, 1)

    row_parts = []
    for lo, hi in spans:
        x = shifted(upstream[0, :, lo:hi], "section", -1)
        from_inner = send(x, INNER_SWAP)
        from_end = send(x, END_TO_FAR)
        local = mm(to_here, x, ((1,), (0,))).astype(bf16)
        near = send(mm(to_mate, x, ((1,), (0,))).astype(bf16), HALF_SWAP)
        relay = [
            send(mm(far_sel[q, 1], got, ((1,), (0,))).astype(bf16), INNER_TO_END)
            for q, got in enumerate((from_inner, from_end))
        ]
        far = [
            (mm(far_sel[q, 0], got, ((1,), (0,))) + relay[q].astype(f32)).astype(bf16)
            for q, got in enumerate((from_inner, from_end))
        ]
        have = [local, near] + far
        kept = [b[:CAP] for b in have]
        given = send(jnp.concatenate([b[CAP:] for b in have], axis=0), CORE_SWAP)
        row_parts.append(jnp.concatenate(kept + [given], axis=0))

    gate_cols, up_cols, down_rows = w_gate[0], w_up[0], w_down[0]
    codes = stash_q[0].reshape(8, CAP, blocks, 128)[order].astype(f32)
    scales = stash_scale[0].reshape(8, CAP, blocks)[order]
    inputs = (codes * scales[..., None]).reshape(8 * CAP, width).astype(bf16)
    gate_pre = mm(inputs, gate_cols, ((1,), (0,)))
    up_pre = mm(inputs, up_cols, ((1,), (0,)))
    sigma = jax.nn.sigmoid(gate_pre)
    swish = gate_pre * sigma
    hidden = swish * up_pre
    scaled_hidden = (weights * hidden).astype(bf16)

    raw_grad = 0.0
    for (lo, hi), part in zip(spans, row_parts):
        raw_grad = raw_grad + mm(part, down_rows[:, lo:hi], ((1,), (1,)))
    gate_part = jnp.sum(hidden * raw_grad, axis=1).reshape(8, CAP)
    grad_hidden = weights * raw_grad
    grad_gate_pre = (grad_hidden * up_pre * sigma * (1.0 + gate_pre * (1.0 - sigma))).astype(bf16)
    grad_up_pre = (grad_hidden * swish).astype(bf16)

    out_parts = []
    half = 4 * CAP
    for lo, hi in spans:
        back = mm(grad_gate_pre, gate_cols[lo:hi], ((1,), (1,)))
        back = (back + mm(grad_up_pre, up_cols[lo:hi], ((1,), (1,)))).astype(bf16)
        other = send(back[half:], CORE_SWAP)
        have = [
            jnp.concatenate([back[CAP * q : CAP * (q + 1)], other[CAP * q : CAP * (q + 1)]], axis=0)
            for q in range(4)
        ]
        relay = [send(have[2 + q], END_TO_INNER) for q in range(2)]
        sums = [
            (mm(far_sel[q, 0], have[2 + q], ((0,), (0,))) + mm(far_sel[q, 1], relay[q], ((0,), (0,)))).astype(bf16)
            for q in range(2)
        ]
        far = send(sums[0], INNER_SWAP).astype(f32) + send(sums[1], FAR_TO_END).astype(f32)
        near = send(have[1], HALF_SWAP)
        total = mm(to_here, have[0], ((0,), (0,))) + mm(to_mate, near, ((0,), (0,))) + far
        out_parts.append(total.astype(bf16))
    grad_input = jnp.concatenate(out_parts, axis=1)

    by_source = jnp.sum(
        jnp.where((order[None, :] == jnp.arange(8)[:, None])[:, :, None], gate_part[None], 0.0),
        axis=1,
    )
    all_parts = gathered(by_source)
    my_parts = jnp.sum(jnp.where((jnp.arange(8) == me)[None, :, None], all_parts, 0.0), axis=1)
    at_expert = jnp.sum(jnp.where(plan[:, None, :] == slot_ids, my_parts[:, :, None], 0.0), axis=1)
    grad_gates = jnp.sum(jnp.where(hit, at_expert[None], 0.0), axis=1).T

    grad_gw = mm(inputs, grad_gate_pre, ((0,), (0,))).astype(bf16)
    grad_uw = mm(inputs, grad_up_pre, ((0,), (0,))).astype(bf16)
    rows = jnp.concatenate(row_parts, axis=1)
    grad_dw = mm(scaled_hidden, rows, ((0,), (0,))).astype(bf16)
    return grad_input[None], grad_gates[None], grad_gw[None], grad_uw[None], grad_dw[None]


def solution(mesh):
    return jax.shard_map(
        relayed if mesh.shape["expert"] == EXPERTS else general,
        mesh=mesh,
        in_specs=(
            P("section", "expert", None),
            P("section", "expert", None),
            P("section", "expert", None),
            P("section", None, "expert"),
            P("section", None, "expert"),
            P("section", "expert", None),
            P("section", "expert", None),
            P("section", "expert", None),
        ),
        out_specs=(
            P("section", "expert", None),
            P("section", "expert", None),
            P("section", None, "expert"),
            P("section", None, "expert"),
            P("section", "expert", None),
        ),
        check_vma=False,
    )
```

```python
import jax
import jax.numpy as jnp
from jax import lax
from jax.experimental import pallas as pl
from jax.experimental.pallas import tpu as pltpu
from jax.sharding import PartitionSpec as P

EXPERT = "expert"
SECTION = "section"
EXPERTS = 8
CAP = 48
OUT_CUTS = (8, 10, 10)
BACK_CUTS = (8, 10, 10)


def shifted(x, axis, by):
    size = lax.axis_size(axis)
    return lax.ppermute(x, axis, [(i, (i + by) % size) for i in range(size)])


def swap(x, bit):
    return lax.ppermute(x, EXPERT, [(i, i ^ bit) for i in range(8)])


def together(*arrays):
    return lax.optimization_barrier(arrays)


def mm(a, b, dims):
    return lax.dot_general(a, b, (dims, ((), ())), preferred_element_type=jnp.float32)


def stacked(*arrays):
    return jnp.concatenate(arrays, axis=0)


def scale_kernel(order, codes, scales, out):
    for b in range(codes.shape[1] // 128):
        at = slice(128 * b, 128 * (b + 1))
        out[:, at] = (codes[:, at].astype(jnp.float32) * scales[:, b : b + 1]).astype(out.dtype)


def scaled_blocks(order, codes, scales):
    count, width = codes.shape
    return pl.pallas_call(
        scale_kernel,
        grid_spec=pltpu.PrefetchScalarGridSpec(
            num_scalar_prefetch=1,
            grid=(count // CAP,),
            in_specs=[
                pl.BlockSpec((CAP, width), lambda i, order: (order[i], 0)),
                pl.BlockSpec((CAP, scales.shape[1]), lambda i, order: (order[i], 0)),
            ],
            out_specs=pl.BlockSpec((CAP, width), lambda i, order: (i, 0)),
        ),
        out_shape=jax.ShapeDtypeStruct((count, width), jnp.bfloat16),
        cost_estimate=pl.CostEstimate(
            flops=count * width, bytes_accessed=4 * count * width, transcendentals=0
        ),
    )(order, codes, scales)


def spans_of(width, cuts):
    blocks, total = width // 128, sum(cuts)
    edges = [128 * (blocks * sum(cuts[:j]) // total) for j in range(len(cuts) + 1)]
    return list(zip(edges[:-1], edges[1:]))


def relayed(upstream, routes, gates, w_gate, w_up, w_down, stash_q, stash_scale):
    bf16, f32 = jnp.bfloat16, jnp.float32
    tokens, width = upstream.shape[1], upstream.shape[2]
    spans, steps = spans_of(width, OUT_CUTS), len(OUT_CUTS)
    me = lax.axis_index(EXPERT)
    gate_cols, up_cols, down_rows = w_gate[0], w_up[0], w_down[0]
    pieces = [upstream[0, :, lo:hi] for lo, hi in spans]
    x = shifted(pieces[0], SECTION, -1)

    route = routes[0].T
    ids = jnp.arange(EXPERTS, dtype=jnp.int32)
    hit = route[:, None, :] == (ids ^ me)[None, :, None]
    named = jnp.any(hit, axis=0)
    earlier = (jnp.arange(tokens)[:, None] < jnp.arange(tokens)[None, :]).astype(bf16)
    plan = jnp.where(named, mm(named.astype(bf16), earlier, ((1,), (0,))), -1.0)
    gate_of = jnp.sum(jnp.where(hit, gates[0].T[:, None, :], 0.0), axis=0)
    slot_ids = jnp.arange(CAP, dtype=f32)[None, :, None]

    def selection(rows):
        return (rows[:, None, :] == slot_ids).astype(bf16).reshape(-1, tokens)

    own_sel = selection(plan[:4])
    both = jnp.stack([plan, gate_of])
    codes = stash_q[0]
    x, both, own_sel, codes, *pieces = together(x, both, own_sel, codes, *pieces)

    def core_part(j):
        return stacked(
            own[j][CAP : 2 * CAP], near_own[j][CAP:], far[j][CAP : 2 * CAP], near_far[j][CAP:]
        )

    own, far, near_own, near_far, parts = {}, {}, {}, {}, {}
    done = {}
    raw_grad = None
    for step in range(steps + 2):
        flying, work = {}, {}
        if step < steps:
            flying["cross"] = swap(x, 4)
        if step + 1 < steps:
            flying["shift"] = shifted(pieces[step + 1], SECTION, -1)
        if step < steps:
            own[step] = mm(own_sel, x, ((1,), (0,))).astype(bf16)
        if 1 <= step <= steps:
            flying["half_far"] = swap(far[step - 1][2 * CAP :], 2)
        if 1 <= step <= steps:
            flying["half_own"] = near_own[step - 1]
        if step < steps:
            near_own[step] = swap(own[step][2 * CAP :], 2)
        if step >= 2:
            flying["core"] = swap(core_part(step - 2), 1)
        if step == 0:
            flying["far_both"] = swap(both, 4)
            order = me ^ jnp.array([0, 2, 4, 6, 1, 3, 5, 7], jnp.int32)
            work["inputs"] = scaled_blocks(order, codes, stash_scale[0])
        if step == 1:
            pair = jnp.stack([both, far_both])
            flying["near_pair"] = swap(pair, 2)
            work["gate"] = mm(inputs, gate_cols, ((1,), (0,)))
            work["up"] = mm(inputs, up_cols, ((1,), (0,)))
        if step == 2:
            quad = jnp.stack([pair, near_pair])
            flying["other_quad"] = swap(quad, 1)
        if step == 3:
            held = jnp.stack([quad, other_quad])
            mine = jnp.stack(
                [held[k & 1, (k >> 1) & 1, k >> 2, :, k] for k in (0, 2, 4, 6, 1, 3, 5, 7)]
            )
            weights = jnp.sum(
                jnp.where(mine[:, 0][:, None, :] == slot_ids, mine[:, 1][:, None, :], 0.0), axis=2
            ).reshape(-1, 1)
            sigma = jax.nn.sigmoid(gate_pre)
            swish = gate_pre * sigma
            work["hidden"] = swish * up_pre
            work["scaled_hidden"] = (weights * work["hidden"]).astype(bf16)
            work["to_gate"] = weights * up_pre * sigma * (1.0 + gate_pre * (1.0 - sigma))
            work["to_up"] = weights * swish
        if step >= 3:
            lo, hi = spans[step - 3]
            more = mm(parts[step - 3], down_rows[:, lo:hi], ((1,), (1,)))
            raw_grad = more if raw_grad is None else raw_grad + more
            work["raw"] = raw_grad
        names, keys = sorted(flying), sorted(work)
        landed = together(*[flying[n] for n in names], *[work[k] for k in keys])
        flying = dict(zip(names, landed))
        work = dict(zip(keys, landed[len(names) :]))
        if "inputs" in work:
            inputs = work["inputs"]
        if "gate" in work:
            gate_pre = work["gate"]
        if "up" in work:
            up_pre = work["up"]
        if "raw" in work:
            raw_grad = work["raw"]
        if "far_both" in flying:
            far_both = flying["far_both"]
            far_sel = selection(far_both[0, 4:])
        if "hidden" in work:
            hidden, scaled_hidden = work["hidden"], work["scaled_hidden"]
            to_gate, to_up = work["to_gate"], work["to_up"]
        if "near_pair" in flying:
            near_pair = flying["near_pair"]
        if "other_quad" in flying:
            other_quad = flying["other_quad"]
        if "cross" in flying:
            far[step] = mm(far_sel, flying["cross"], ((1,), (0,))).astype(bf16)
        if "shift" in flying:
            x = flying["shift"]
        if "half_far" in flying:
            near_far[step - 1] = flying["half_far"]
        if "half_own" in flying:
            near_own[step - 1] = flying["half_own"]
        if "core" in flying:
            j = step - 2
            parts[j] = stacked(
                own[j][:CAP], near_own[j][:CAP], far[j][:CAP], near_far[j][:CAP], flying["core"]
            )

    for j in range(steps):
        lo, hi = spans[j]
        if j >= steps - 1:
            raw_grad = raw_grad + mm(parts[j], down_rows[:, lo:hi], ((1,), (1,)))
    grad_gate_pre = (raw_grad * to_gate).astype(bf16)
    grad_up_pre = (raw_grad * to_up).astype(bf16)

    spans, steps = spans_of(width, BACK_CUTS), len(BACK_CUTS)

    def back_of(j, ggp, gup):
        lo, hi = spans[j]
        back = mm(ggp, gate_cols[lo:hi], ((1,), (1,)))
        return (back + mm(gup, up_cols[lo:hi], ((1,), (1,)))).astype(bf16)

    ggp, gup = grad_gate_pre, grad_up_pre
    back = {0: back_of(0, ggp, gup)}
    rest = [ggp, gup, inputs, raw_grad, hidden] + [parts[j] for j in sorted(parts)]
    back[0], *rest = together(back[0], *rest)
    far, own, near_far, near_own, out, mates, crossed = {}, {}, {}, {}, {}, {}, {}
    for step in range(steps + 2):
        flying, work = {}, {}
        ggp, gup, inputs, raw_grad, hidden = rest[:5]
        if step < steps:
            flying["core"] = swap(back[step][4 * CAP :], 1)
        if 0 <= step - 1 < steps:
            flying["half_far"] = swap(far[step - 1], 2)
        if 0 <= step - 2 < steps:
            flying["cross"] = swap(out[step - 2], 4)
            near_own[step - 2] = swap(mates[step - 2], 2)
        if 0 <= step - 3 < steps:
            flying["half_own"] = near_own[step - 3]
        if step + 1 < steps:
            work["back"] = back_of(step + 1, ggp, gup)
        if step == 1:
            gate_part = jnp.sum(hidden * raw_grad, axis=1).reshape(8, CAP)
            work["spread"] = jnp.stack([gate_part[i] for i in (0, 4, 1, 5, 2, 6, 3, 7)])[None]
        if 2 <= step <= 4:
            bit = 1 << (step - 2)
            flying["spread"] = swap(spread, bit)
        if step == steps - 1:
            work["gw"] = mm(inputs, ggp, ((0,), (0,))).astype(bf16)
        if step == steps:
            work["uw"] = mm(inputs, gup, ((0,), (0,))).astype(bf16)
        if step == steps + 1:
            work["dw"] = mm(scaled_hidden, jnp.concatenate(rest[5:], axis=1), ((0,), (0,))).astype(bf16)
        names, keys = sorted(flying), sorted(work)
        landed = together(*[flying[n] for n in names], *[work[k] for k in keys], *rest)
        flying = dict(zip(names, landed))
        work = dict(zip(keys, landed[len(names) :]))
        rest = landed[len(names) + len(keys) :]
        if "back" in work:
            back[step + 1] = work["back"]
        if "spread" in work:
            spread = work["spread"]
        if "spread" in flying:
            got = flying["spread"]
            got = got.reshape((got.shape[0], 8 // (2 * bit), 2, bit, CAP))[:, :, ::-1].reshape(got.shape)
            spread = jnp.concatenate([spread, got], axis=0)
        if "gw" in work:
            grad_gw = work["gw"]
        if "uw" in work:
            grad_uw = work["uw"]
        if "dw" in work:
            grad_dw = work["dw"]
        if "core" in flying:
            mine_b, oth = back[step], flying["core"]
            own[step], mates[step], near_far[step], far[step] = [
                stacked(mine_b[CAP * q : CAP * (q + 1)], oth[CAP * q : CAP * (q + 1)]) for q in range(4)
            ]
        if "half_far" in flying:
            k = step - 1
            out[k] = mm(far_sel, stacked(near_far[k], flying["half_far"]), ((0,), (0,))).astype(bf16)
        if "half_own" in flying:
            k = step - 3
            near_own[k] = flying["half_own"]
            own_sum = mm(own_sel, stacked(own[k], near_own[k]), ((0,), (0,)))
            out[k] = (own_sum + crossed[k].astype(f32)).astype(bf16)
        if "cross" in flying:
            crossed[step - 2] = flying["cross"]
            if step - 2 == steps - 1:
                k = step - 2
                own_sum = mm(own_sel, stacked(own[k], near_own[k]), ((0,), (0,)))
                out[k] = (own_sum + crossed[k].astype(f32)).astype(bf16)
    grad_input = jnp.concatenate([out[k] for k in range(steps)], axis=1)

    mine_parts = spread[:, 0]
    at_expert = jnp.sum(jnp.where(plan[:, None, :] == slot_ids, mine_parts[:, :, None], 0.0), axis=1)
    grad_gates = jnp.sum(jnp.where(hit, at_expert[None], 0.0), axis=1).T
    return grad_input[None], grad_gates[None], grad_gw[None], grad_uw[None], grad_dw[None]


def slot_work(codes, scales, cotangent, weights, gate_cols, up_cols, down_rows):
    count, width = codes.shape
    blocks = width // 128
    inputs = (
        (codes.astype(jnp.float32).reshape(count, blocks, 128) * scales[:, :, None])
        .reshape(count, width)
        .astype(jnp.bfloat16)
    )
    gate_pre = jnp.dot(inputs, gate_cols, preferred_element_type=jnp.float32)
    up_pre = jnp.dot(inputs, up_cols, preferred_element_type=jnp.float32)
    sigma = jax.nn.sigmoid(gate_pre)
    swish = gate_pre * sigma
    hidden = swish * up_pre
    scaled_hidden = (weights[:, None] * hidden).astype(jnp.bfloat16)
    grad_down = lax.dot_general(
        scaled_hidden, cotangent, (((0,), (0,)), ((), ())), preferred_element_type=jnp.float32
    )
    raw_grad = lax.dot_general(
        cotangent, down_rows, (((1,), (1,)), ((), ())), preferred_element_type=jnp.float32
    )
    gate_part = jnp.sum(hidden * raw_grad, axis=1)
    grad_hidden = weights[:, None] * raw_grad
    grad_gate_pre = (grad_hidden * up_pre * sigma * (1.0 + gate_pre * (1.0 - sigma))).astype(
        jnp.bfloat16
    )
    grad_up_pre = (grad_hidden * swish).astype(jnp.bfloat16)
    grad_gate_w = lax.dot_general(
        inputs, grad_gate_pre, (((0,), (0,)), ((), ())), preferred_element_type=jnp.float32
    )
    grad_up_w = lax.dot_general(
        inputs, grad_up_pre, (((0,), (0,)), ((), ())), preferred_element_type=jnp.float32
    )
    input_sum = lax.dot_general(
        grad_gate_pre, gate_cols, (((1,), (1,)), ((), ())), preferred_element_type=jnp.float32
    )
    input_sum = input_sum + lax.dot_general(
        grad_up_pre, up_cols, (((1,), (1,)), ((), ())), preferred_element_type=jnp.float32
    )
    return (grad_gate_w, grad_up_w, grad_down, input_sum.astype(jnp.bfloat16), gate_part)


def general(upstream, routes, gates, w_gate, w_up, w_down, stash_q, stash_scale):
    cotangent = shifted(upstream[0], SECTION, -1)
    tok_dev = routes.shape[1]
    topk = routes.shape[2]
    width = cotangent.shape[1]
    groups = lax.axis_size(EXPERT)
    hsplit = groups // EXPERTS
    slots = groups * CAP
    flat = routes[0].reshape(-1)
    onehot = (flat[:, None] == jnp.arange(EXPERTS, dtype=jnp.int32)[None, :]).astype(jnp.int32)
    before = jnp.cumsum(onehot, axis=0) - onehot
    slot = jnp.sum(before * onehot, axis=1)
    target = flat * CAP + slot
    token = jnp.arange(tok_dev * topk, dtype=jnp.int32) // topk
    row_buf = jnp.zeros((EXPERTS * CAP, width), jnp.bfloat16).at[target].set(cotangent[token])
    weight_buf = jnp.zeros((EXPERTS * CAP,), jnp.float32).at[target].set(gates[0].reshape(-1))
    send_rows = jnp.repeat(row_buf.reshape(EXPERTS, CAP, width), hsplit, axis=0)
    send_weights = jnp.repeat(weight_buf.reshape(EXPERTS, CAP), hsplit, axis=0)
    got_rows, got_weights = (
        lax.all_to_all(send_rows, EXPERT, split_axis=0, concat_axis=0, tiled=True),
        lax.all_to_all(
            send_weights.astype(jnp.bfloat16), EXPERT, split_axis=0, concat_axis=0, tiled=True
        ).astype(send_weights.dtype),
    )
    rows = got_rows.reshape(slots, width)
    weights = got_weights.reshape(slots)
    grad_gw, grad_uw, grad_dw, input_part, gate_part = slot_work(
        stash_q[0], stash_scale[0], rows, weights, w_gate[0], w_up[0], w_down[0]
    )
    back_rows, back_gates = (
        lax.all_to_all(
            input_part.reshape(groups, CAP, width), EXPERT, split_axis=0, concat_axis=0, tiled=True
        ),
        lax.all_to_all(
            gate_part.reshape(groups, CAP).astype(jnp.bfloat16),
            EXPERT,
            split_axis=0,
            concat_axis=0,
            tiled=True,
        ).astype(jnp.float32),
    )
    summed = jnp.sum(
        back_rows.reshape(EXPERTS, hsplit, CAP, width).astype(jnp.float32), axis=1
    ).reshape(EXPERTS * CAP, width)
    gate_sum = jnp.sum(
        back_gates.reshape(EXPERTS, hsplit, CAP).astype(jnp.float32), axis=1
    ).reshape(EXPERTS * CAP)
    grad_input = jnp.sum(summed[target].reshape(tok_dev, topk, width), axis=1).astype(jnp.bfloat16)
    grad_gates = gate_sum[target].reshape(tok_dev, topk)
    return (
        grad_input[None],
        grad_gates[None],
        grad_gw.astype(jnp.bfloat16)[None],
        grad_uw.astype(jnp.bfloat16)[None],
        grad_dw.astype(jnp.bfloat16)[None],
    )


def solution(mesh):
    return jax.shard_map(
        relayed if mesh.shape[EXPERT] == EXPERTS else general,
        mesh=mesh,
        in_specs=(
            P(SECTION, EXPERT, None),
            P(SECTION, EXPERT, None),
            P(SECTION, EXPERT, None),
            P(SECTION, None, EXPERT),
            P(SECTION, None, EXPERT),
            P(SECTION, EXPERT, None),
            P(SECTION, EXPERT, None),
            P(SECTION, EXPERT, None),
        ),
        out_specs=(
            P(SECTION, EXPERT, None),
            P(SECTION, EXPERT, None),
            P(SECTION, None, EXPERT),
            P(SECTION, None, EXPERT),
            P(SECTION, EXPERT, None),
        ),
        check_vma=False,
    )
```

```python
import jax
import jax.numpy as jnp
from jax import lax
from jax.experimental import pallas as pl
from jax.experimental.pallas import tpu as pltpu
from jax.sharding import PartitionSpec as P

EXPERT = "expert"
SECTION = "section"
EXPERTS = 8
CAP = 48
OUT_CUTS = (10, 18)
BACK_CUTS = (10, 18)


def shifted(x, axis, by):
    size = lax.axis_size(axis)
    return lax.ppermute(x, axis, [(i, (i + by) % size) for i in range(size)])


def swap(x, bit):
    return lax.ppermute(x, EXPERT, [(i, i ^ bit) for i in range(8)])


def together(*arrays):
    return lax.optimization_barrier(arrays)


def mm(a, b, dims):
    return lax.dot_general(a, b, (dims, ((), ())), preferred_element_type=jnp.float32)


def stacked(*arrays):
    return jnp.concatenate(arrays, axis=0)


def scale_kernel(order, *refs):
    *pairs, out = refs
    for j in range(len(pairs) // 2):
        codes, scales = pairs[2 * j], pairs[2 * j + 1]
        rows = slice(CAP * j, CAP * (j + 1))
        for b in range(codes.shape[1] // 128):
            at = slice(128 * b, 128 * (b + 1))
            got = codes[:, at].astype(jnp.float32) * scales[:, b : b + 1]
            out[rows, at] = got.astype(out.dtype)


def scaled_blocks(order, codes, scales):
    count, width = codes.shape
    at_once = 4
    specs = []
    for j in range(at_once):
        specs.append(pl.BlockSpec((CAP, width), lambda i, order, j=j: (order[at_once * i + j], 0)))
        specs.append(
            pl.BlockSpec((CAP, scales.shape[1]), lambda i, order, j=j: (order[at_once * i + j], 0))
        )
    return pl.pallas_call(
        scale_kernel,
        grid_spec=pltpu.PrefetchScalarGridSpec(
            num_scalar_prefetch=1,
            grid=(count // CAP // at_once,),
            in_specs=specs,
            out_specs=pl.BlockSpec((CAP * at_once, width), lambda i, order: (i, 0)),
        ),
        out_shape=jax.ShapeDtypeStruct((count, width), jnp.bfloat16),
        compiler_params=pltpu.CompilerParams(vmem_limit_bytes=24 * 2**20),
        cost_estimate=pl.CostEstimate(
            flops=count * width, bytes_accessed=4 * count * width, transcendentals=0
        ),
    )(order, *[codes, scales] * at_once)


def spans_of(width, cuts):
    blocks, total = width // 128, sum(cuts)
    edges = [128 * (blocks * sum(cuts[:j]) // total) for j in range(len(cuts) + 1)]
    return list(zip(edges[:-1], edges[1:]))


def relayed(upstream, routes, gates, w_gate, w_up, w_down, stash_q, stash_scale):
    bf16, f32 = jnp.bfloat16, jnp.float32
    tokens, width = upstream.shape[1], upstream.shape[2]
    spans, steps = spans_of(width, OUT_CUTS), len(OUT_CUTS)
    half = 4 * CAP
    me = lax.axis_index(EXPERT)
    gate_cols, up_cols, down_rows = w_gate[0], w_up[0], w_down[0]
    codes, scales = stash_q[0], stash_scale[0]
    pieces = [upstream[0, :, lo:hi] for lo, hi in spans]
    xs = [shifted(pieces[0], SECTION, -1)]

    route = routes[0].T
    ids = jnp.arange(EXPERTS, dtype=jnp.int32)
    hit = route[:, None, :] == (ids ^ me)[None, :, None]
    named = jnp.any(hit, axis=0)
    earlier = (jnp.arange(tokens)[:, None] < jnp.arange(tokens)[None, :]).astype(bf16)
    plan = jnp.where(named, mm(named.astype(bf16), earlier, ((1,), (0,))), -1.0)
    gate_of = jnp.sum(jnp.where(hit, gates[0].T[:, None, :], 0.0), axis=0)
    slot_ids = jnp.arange(CAP, dtype=f32)[None, :, None]

    def selection(rows):
        return (rows[:, None, :] == slot_ids).astype(bf16).reshape(-1, tokens)

    def traded(name, rows, which):
        got = {}
        for m in which:
            got[m] = swap(rows[CAP * m : CAP * (m + 1)], m)
        return got

    def pack(sel, rows):
        return mm(sel, rows, ((1,), (0,))).astype(bf16)

    def pieces_of(values):
        got = []
        for _ in range(3):
            got.append(lax.reduce_precision(values, 8, 7))
            values = values - got[-1]
        return jnp.stack(got, axis=-1).astype(bf16)

    def gate_columns(table):
        columns = pieces_of(table).transpose(1, 0, 2).reshape(tokens, -1)
        return jnp.pad(columns, ((0, 0), (0, 128 - columns.shape[1])))

    near_sel = selection(plan[:4])
    both = jnp.stack([plan, gate_of])
    x, pieces, near_sel, both, codes, scales = together(
        xs[0], pieces, near_sel, both, codes, scales
    )

    cross = swap(x, 4)
    x1 = shifted(pieces[1], SECTION, -1)
    own = jnp.concatenate([pack(near_sel, x), pack(near_sel, gate_columns(both[1, :4]))], axis=1)
    own, both, codes = together(own, both, codes)
    near_own = swap(own[2 * CAP :], 2)
    far_both = swap(both, 4)
    inputs = scaled_blocks(me ^ jnp.arange(8, dtype=jnp.int32), codes, scales)
    cross, x, own, near_own, far_both, inputs = together(cross, x1, own, near_own, far_both, inputs)

    next_cross = swap(x, 4)
    far_sel = selection(far_both[0, 4:])
    far = [pack(far_sel, cross), pack(far_sel, gate_columns(far_both[1, 4:]))]
    far = jnp.concatenate(far, axis=1)
    far, x, own, near_own, inputs = together(far, x, own, near_own, inputs)
    near_far = swap(far[2 * CAP :], 2)
    own_1 = pack(near_sel, x)
    own_1, own, near_own, inputs = together(own_1, own, near_own, inputs)
    near_own_1 = swap(own_1[2 * CAP :], 2)
    given = swap(stacked(own[CAP : 2 * CAP], near_own[CAP:]), 1)
    gate_pre = mm(inputs, gate_cols, ((1,), (0,)))
    up_pre = mm(inputs, up_cols, ((1,), (0,)))
    near_rows = stacked(own[:CAP], given[:CAP], near_own[:CAP], given[CAP:])
    cross, near_far, near_own_1, near_rows, gate_pre, up_pre, far, own_1 = together(
        next_cross, near_far, near_own_1, near_rows, gate_pre, up_pre, far, own_1
    )

    far_1 = pack(far_sel, cross)
    far_1, far, near_far, own_1, near_own_1, near_rows = together(
        far_1, far, near_far, own_1, near_own_1, near_rows
    )
    got = traded("far_1", far_1, (2, 3, 1))
    given = swap(stacked(far[CAP : 2 * CAP], near_far[CAP:]), 1)
    given_1 = swap(stacked(own_1[CAP : 2 * CAP], near_own_1[CAP:]), 1)
    rows = stacked(near_rows, far[:CAP], given[:CAP], near_far[:CAP], given[CAP:])
    lo = spans[1][0]
    wanted = jnp.arange(128)[None, :] // 3 == jnp.arange(8 * CAP)[:, None] // CAP % 4
    weights = jnp.sum(jnp.where(wanted, rows[:, lo:].astype(f32), 0.0), axis=1, keepdims=True)
    parts = [rows[:, :lo]]
    raw_grad = mm(parts[0], down_rows[:, :lo], ((1,), (1,)))
    sigma = jax.nn.sigmoid(gate_pre)
    swish = gate_pre * sigma
    hidden = swish * up_pre
    scaled_hidden = (weights * hidden).astype(bf16)
    to_gate = weights * up_pre * sigma * (1.0 + gate_pre * (1.0 - sigma))
    to_up = weights * swish
    got, given_1, parts, raw_grad, hidden, scaled_hidden, to_gate, to_up = together(
        got, given_1, parts, raw_grad, hidden, scaled_hidden, to_gate, to_up
    )
    parts.append(
        stacked(
            own_1[:CAP], given_1[:CAP], near_own_1[:CAP], given_1[CAP:], far_1[:CAP], got[1], got[2], got[3]
        )
    )
    raw_grad = raw_grad + mm(parts[1], down_rows[:, lo:], ((1,), (1,)))
    grad_gate_pre = (raw_grad * to_gate).astype(bf16)
    grad_up_pre = (raw_grad * to_up).astype(bf16)

    spans, steps = spans_of(width, BACK_CUTS), len(BACK_CUTS)
    column = jnp.arange(128, dtype=jnp.int32)[None, :]

    def back_of(j, ggp, gup):
        lo, hi = spans[j]
        back = mm(ggp, gate_cols[lo:hi], ((1,), (1,)))
        return (back + mm(gup, up_cols[lo:hi], ((1,), (1,)))).astype(bf16)

    def gate_terms(hidden, raw_grad):
        left = jnp.sum(hidden * raw_grad, axis=1, keepdims=True)
        terms = jnp.zeros((left.shape[0], 128), f32)
        for i in range(3):
            piece = lax.reduce_precision(left, 8, 7)
            terms = jnp.where(column == 3 * me + i, piece, terms)
            left = left - piece
        return terms.astype(bf16)

    def far_hands(j):
        got = traded(f"rfar_{j}", back[j][half:], (2, 3, 1))
        return [back[j][half : half + CAP]] + [got[m] for m in (1, 2, 3)]

    rest = (grad_gate_pre, grad_up_pre, inputs, raw_grad, hidden, scaled_hidden, parts)
    back = {0: back_of(0, grad_gate_pre, grad_up_pre)}
    back[0], rest = together(back[0], rest)
    hands = far_hands(0)
    back[1] = back_of(1, *rest[:2])
    back[1] = jnp.concatenate([back[1], gate_terms(rest[4], rest[3])], axis=1)
    near_back = jnp.concatenate([back[j][:half] for j in range(steps)], axis=1)
    hands, back, rest, near_back = together(hands, back, rest, near_back)

    def crossing(name, hands):
        far_sum = mm(far_sel, stacked(*hands), ((0,), (0,))).astype(bf16)
        return far_sum

    more = far_hands(1)
    far_sum = crossing(0, hands)
    far_sum, rest, near_back = together(far_sum, rest, near_back)
    crossed = [swap(far_sum, 4)]
    near = traded("rnear", near_back, (2,))
    grad_gw = mm(rest[2], rest[0], ((0,), (0,))).astype(bf16)
    hands, grad_gw, rest, near_back = together(more, grad_gw, rest, near_back)
    far_sum = crossing(1, hands)
    far_sum, rest, near_back = together(far_sum, rest, near_back)
    crossed.append(swap(far_sum, 4))
    near.update(traded("rnear", near_back, (3, 1)))
    grad_uw = mm(rest[2], rest[1], ((0,), (0,))).astype(bf16)
    grad_dw = mm(rest[5], jnp.concatenate(rest[6], axis=1), ((0,), (0,))).astype(bf16)
    total = mm(near_sel, stacked(near_back[:CAP], near[1], near[2], near[3]), ((0,), (0,)))
    total = (total + jnp.concatenate(crossed, axis=1).astype(f32)).astype(bf16)
    terms, grad_input = total[:, width:].astype(f32), total[:, :width]
    wanted = column[None] // 3 == routes[0][:, :, None]
    grad_gates = jnp.sum(jnp.where(wanted, terms[:, None, :], 0.0), axis=2)
    return grad_input[None], grad_gates[None], grad_gw[None], grad_uw[None], grad_dw[None]


def slot_work(codes, scales, cotangent, weights, gate_cols, up_cols, down_rows):
    count, width = codes.shape
    blocks = width // 128
    inputs = (
        (codes.astype(jnp.float32).reshape(count, blocks, 128) * scales[:, :, None])
        .reshape(count, width)
        .astype(jnp.bfloat16)
    )
    gate_pre = jnp.dot(inputs, gate_cols, preferred_element_type=jnp.float32)
    up_pre = jnp.dot(inputs, up_cols, preferred_element_type=jnp.float32)
    sigma = jax.nn.sigmoid(gate_pre)
    swish = gate_pre * sigma
    hidden = swish * up_pre
    scaled_hidden = (weights[:, None] * hidden).astype(jnp.bfloat16)
    grad_down = lax.dot_general(
        scaled_hidden, cotangent, (((0,), (0,)), ((), ())), preferred_element_type=jnp.float32
    )
    raw_grad = lax.dot_general(
        cotangent, down_rows, (((1,), (1,)), ((), ())), preferred_element_type=jnp.float32
    )
    gate_part = jnp.sum(hidden * raw_grad, axis=1)
    grad_hidden = weights[:, None] * raw_grad
    grad_gate_pre = (grad_hidden * up_pre * sigma * (1.0 + gate_pre * (1.0 - sigma))).astype(
        jnp.bfloat16
    )
    grad_up_pre = (grad_hidden * swish).astype(jnp.bfloat16)
    grad_gate_w = lax.dot_general(
        inputs, grad_gate_pre, (((0,), (0,)), ((), ())), preferred_element_type=jnp.float32
    )
    grad_up_w = lax.dot_general(
        inputs, grad_up_pre, (((0,), (0,)), ((), ())), preferred_element_type=jnp.float32
    )
    input_sum = lax.dot_general(
        grad_gate_pre, gate_cols, (((1,), (1,)), ((), ())), preferred_element_type=jnp.float32
    )
    input_sum = input_sum + lax.dot_general(
        grad_up_pre, up_cols, (((1,), (1,)), ((), ())), preferred_element_type=jnp.float32
    )
    return (grad_gate_w, grad_up_w, grad_down, input_sum.astype(jnp.bfloat16), gate_part)


def general(upstream, routes, gates, w_gate, w_up, w_down, stash_q, stash_scale):
    cotangent = shifted(upstream[0], SECTION, -1)
    tok_dev = routes.shape[1]
    topk = routes.shape[2]
    width = cotangent.shape[1]
    groups = lax.axis_size(EXPERT)
    hsplit = groups // EXPERTS
    slots = groups * CAP
    flat = routes[0].reshape(-1)
    onehot = (flat[:, None] == jnp.arange(EXPERTS, dtype=jnp.int32)[None, :]).astype(jnp.int32)
    before = jnp.cumsum(onehot, axis=0) - onehot
    slot = jnp.sum(before * onehot, axis=1)
    target = flat * CAP + slot
    token = jnp.arange(tok_dev * topk, dtype=jnp.int32) // topk
    row_buf = jnp.zeros((EXPERTS * CAP, width), jnp.bfloat16).at[target].set(cotangent[token])
    weight_buf = jnp.zeros((EXPERTS * CAP,), jnp.float32).at[target].set(gates[0].reshape(-1))
    send_rows = jnp.repeat(row_buf.reshape(EXPERTS, CAP, width), hsplit, axis=0)
    send_weights = jnp.repeat(weight_buf.reshape(EXPERTS, CAP), hsplit, axis=0)
    got_rows, got_weights = (
        lax.all_to_all(send_rows, EXPERT, split_axis=0, concat_axis=0, tiled=True),
        lax.all_to_all(
            send_weights.astype(jnp.bfloat16), EXPERT, split_axis=0, concat_axis=0, tiled=True
        ).astype(send_weights.dtype),
    )
    rows = got_rows.reshape(slots, width)
    weights = got_weights.reshape(slots)
    grad_gw, grad_uw, grad_dw, input_part, gate_part = slot_work(
        stash_q[0], stash_scale[0], rows, weights, w_gate[0], w_up[0], w_down[0]
    )
    back_rows, back_gates = (
        lax.all_to_all(
            input_part.reshape(groups, CAP, width), EXPERT, split_axis=0, concat_axis=0, tiled=True
        ),
        lax.all_to_all(
            gate_part.reshape(groups, CAP).astype(jnp.bfloat16),
            EXPERT,
            split_axis=0,
            concat_axis=0,
            tiled=True,
        ).astype(jnp.float32),
    )
    summed = jnp.sum(
        back_rows.reshape(EXPERTS, hsplit, CAP, width).astype(jnp.float32), axis=1
    ).reshape(EXPERTS * CAP, width)
    gate_sum = jnp.sum(
        back_gates.reshape(EXPERTS, hsplit, CAP).astype(jnp.float32), axis=1
    ).reshape(EXPERTS * CAP)
    grad_input = jnp.sum(summed[target].reshape(tok_dev, topk, width), axis=1).astype(jnp.bfloat16)
    grad_gates = gate_sum[target].reshape(tok_dev, topk)
    return (
        grad_input[None],
        grad_gates[None],
        grad_gw.astype(jnp.bfloat16)[None],
        grad_uw.astype(jnp.bfloat16)[None],
        grad_dw.astype(jnp.bfloat16)[None],
    )


def solution(mesh):
    return jax.shard_map(
        relayed if mesh.shape[EXPERT] == EXPERTS else general,
        mesh=mesh,
        in_specs=(
            P(SECTION, EXPERT, None),
            P(SECTION, EXPERT, None),
            P(SECTION, EXPERT, None),
            P(SECTION, None, EXPERT),
            P(SECTION, None, EXPERT),
            P(SECTION, EXPERT, None),
            P(SECTION, EXPERT, None),
            P(SECTION, EXPERT, None),
        ),
        out_specs=(
            P(SECTION, EXPERT, None),
            P(SECTION, EXPERT, None),
            P(SECTION, None, EXPERT),
            P(SECTION, None, EXPERT),
            P(SECTION, EXPERT, None),
        ),
        check_vma=False,
    )
```

```python
import jax
import jax.numpy as jnp
from jax import lax
from jax.experimental import pallas as pl
from jax.experimental.pallas import tpu as pltpu
from jax.sharding import PartitionSpec as P

EXPERT = "expert"
SECTION = "section"
EXPERTS = 8
CAP = 48
OUT_CUTS = (7, 21)
BACK_CUTS = (10, 18)


def shifted(x, axis, by):
    size = lax.axis_size(axis)
    return lax.ppermute(x, axis, [(i, (i + by) % size) for i in range(size)])


def swap(x, bit):
    return lax.ppermute(x, EXPERT, [(i, i ^ bit) for i in range(8)])


def together(*arrays):
    return lax.optimization_barrier(arrays)


def mm(a, b, dims):
    return lax.dot_general(a, b, (dims, ((), ())), preferred_element_type=jnp.float32)


def stacked(*arrays):
    return jnp.concatenate(arrays, axis=0)


def scale_kernel(order, *refs):
    *pairs, out = refs
    for j in range(len(pairs) // 2):
        codes, scales = pairs[2 * j], pairs[2 * j + 1]
        rows = slice(CAP * j, CAP * (j + 1))
        for b in range(codes.shape[1] // 128):
            at = slice(128 * b, 128 * (b + 1))
            got = codes[:, at].astype(jnp.float32) * scales[:, b : b + 1]
            out[rows, at] = got.astype(out.dtype)


def scaled_blocks(order, codes, scales):
    count, width = codes.shape
    at_once = 4
    specs = []
    for j in range(at_once):
        specs.append(pl.BlockSpec((CAP, width), lambda i, order, j=j: (order[at_once * i + j], 0)))
        specs.append(
            pl.BlockSpec((CAP, scales.shape[1]), lambda i, order, j=j: (order[at_once * i + j], 0))
        )
    return pl.pallas_call(
        scale_kernel,
        grid_spec=pltpu.PrefetchScalarGridSpec(
            num_scalar_prefetch=1,
            grid=(count // CAP // at_once,),
            in_specs=specs,
            out_specs=pl.BlockSpec((CAP * at_once, width), lambda i, order: (i, 0)),
        ),
        out_shape=jax.ShapeDtypeStruct((count, width), jnp.bfloat16),
        compiler_params=pltpu.CompilerParams(vmem_limit_bytes=24 * 2**20),
        cost_estimate=pl.CostEstimate(
            flops=1, bytes_accessed=1, transcendentals=0
        ),
    )(order, *[codes, scales] * at_once)


def spans_of(width, cuts):
    blocks, total = width // 128, sum(cuts)
    edges = [128 * (blocks * sum(cuts[:j]) // total) for j in range(len(cuts) + 1)]
    return list(zip(edges[:-1], edges[1:]))


def relayed(upstream, routes, gates, w_gate, w_up, w_down, stash_q, stash_scale):
    bf16, f32 = jnp.bfloat16, jnp.float32
    tokens, width = upstream.shape[1], upstream.shape[2]
    spans, steps = spans_of(width, OUT_CUTS), len(OUT_CUTS)
    half = 4 * CAP
    me = lax.axis_index(EXPERT)
    gate_cols, up_cols, down_rows = w_gate[0], w_up[0], w_down[0]
    codes, scales = stash_q[0], stash_scale[0]
    pieces = [upstream[0, :, lo:hi] for lo, hi in spans]
    xs = [shifted(pieces[0], SECTION, -1)]
    x1 = shifted(pieces[1], SECTION, -1)

    route = routes[0].T
    ids = jnp.arange(EXPERTS, dtype=jnp.int32)
    hit = route[:, None, :] == (ids ^ me)[None, :, None]
    named = jnp.any(hit, axis=0)
    earlier = (jnp.arange(tokens)[:, None] < jnp.arange(tokens)[None, :]).astype(bf16)
    plan = jnp.where(named, mm(named.astype(bf16), earlier, ((1,), (0,))), -1.0)
    gate_of = jnp.sum(jnp.where(hit, gates[0].T[:, None, :], 0.0), axis=0)
    slot_ids = jnp.arange(CAP, dtype=f32)[None, :, None]

    def selection(rows):
        return (rows[:, None, :] == slot_ids).astype(bf16).reshape(-1, tokens)

    def traded(name, rows, which):
        got = {}
        for m in which:
            got[m] = swap(rows[CAP * m : CAP * (m + 1)], m)
        return got

    def pack(sel, rows):
        return mm(sel, rows, ((1,), (0,))).astype(bf16)

    def pieces_of(values):
        got = []
        for _ in range(3):
            got.append(lax.reduce_precision(values, 8, 7))
            values = values - got[-1]
        return jnp.stack(got, axis=-1).astype(bf16)

    def gate_columns(table):
        columns = pieces_of(table).transpose(1, 0, 2).reshape(tokens, -1)
        return jnp.pad(columns, ((0, 0), (0, 128 - columns.shape[1])))

    near_sel = selection(plan[:4])
    both = jnp.stack([plan, gate_of])
    x, pieces, near_sel, both, codes, scales = together(
        xs[0], pieces, near_sel, both, codes, scales
    )

    cross = swap(x, 4)
    own = jnp.concatenate([pack(near_sel, x), pack(near_sel, gate_columns(both[1, :4]))], axis=1)
    own, both, codes = together(own, both, codes)
    near_own = swap(own[2 * CAP :], 2)
    far_both = swap(both, 4)
    inputs = scaled_blocks(me ^ jnp.arange(8, dtype=jnp.int32), codes, scales)
    far_sel = selection(far_both[0, 4:])
    gates_far = pack(far_sel, gate_columns(far_both[1, 4:]))
    cross, x, own, near_own, far_sel, gates_far, inputs = together(
        cross, x1, own, near_own, far_sel, gates_far, inputs
    )

    next_cross = swap(x, 4)
    far = jnp.concatenate([pack(far_sel, cross), gates_far], axis=1)
    far, x, own, near_own, inputs = together(far, x, own, near_own, inputs)
    near_far = swap(far[2 * CAP :], 2)
    own_1 = pack(near_sel, x)
    own_1, own, near_own, inputs = together(own_1, own, near_own, inputs)
    near_own_1 = swap(own_1[2 * CAP :], 2)
    given = swap(stacked(own[CAP : 2 * CAP], near_own[CAP:]), 1)
    gate_pre = mm(inputs, gate_cols, ((1,), (0,)))
    up_pre = mm(inputs, up_cols, ((1,), (0,)))
    near_rows = stacked(own[:CAP], given[:CAP], near_own[:CAP], given[CAP:])
    cross, near_far, near_own_1, near_rows, gate_pre, up_pre, far, own_1 = together(
        next_cross, near_far, near_own_1, near_rows, gate_pre, up_pre, far, own_1
    )

    far_1 = pack(far_sel, cross)
    far_1, far, near_far, own_1, near_own_1, near_rows = together(
        far_1, far, near_far, own_1, near_own_1, near_rows
    )
    got = traded("far_1", far_1, (2, 3, 1))
    given = swap(stacked(far[CAP : 2 * CAP], near_far[CAP:]), 1)
    given_1 = swap(stacked(own_1[CAP : 2 * CAP], near_own_1[CAP:]), 1)
    rows = stacked(near_rows, far[:CAP], given[:CAP], near_far[:CAP], given[CAP:])
    lo = spans[1][0]
    wanted = jnp.arange(128)[None, :] // 3 == jnp.arange(8 * CAP)[:, None] // CAP % 4
    weights = jnp.sum(jnp.where(wanted, rows[:, lo:].astype(f32), 0.0), axis=1, keepdims=True)
    parts = [rows[:, :lo]]
    raw_grad = mm(parts[0], down_rows[:, :lo], ((1,), (1,)))
    sigma = jax.nn.sigmoid(gate_pre)
    swish = gate_pre * sigma
    hidden = swish * up_pre
    scaled_hidden = (weights * hidden).astype(bf16)
    to_gate = weights * up_pre * sigma * (1.0 + gate_pre * (1.0 - sigma))
    to_up = weights * swish
    got, given_1, parts, raw_grad, hidden, scaled_hidden, to_gate, to_up = together(
        got, given_1, parts, raw_grad, hidden, scaled_hidden, to_gate, to_up
    )
    parts.append(
        stacked(
            own_1[:CAP], given_1[:CAP], near_own_1[:CAP], given_1[CAP:], far_1[:CAP], got[1], got[2], got[3]
        )
    )
    raw_grad = raw_grad + mm(parts[1], down_rows[:, lo:], ((1,), (1,)))
    grad_gate_pre = (raw_grad * to_gate).astype(bf16)
    grad_up_pre = (raw_grad * to_up).astype(bf16)

    spans, steps = spans_of(width, BACK_CUTS), len(BACK_CUTS)
    column = jnp.arange(128, dtype=jnp.int32)[None, :]

    def back_of(j, ggp, gup):
        lo, hi = spans[j]
        back = mm(ggp, gate_cols[lo:hi], ((1,), (1,)))
        return (back + mm(gup, up_cols[lo:hi], ((1,), (1,)))).astype(bf16)

    def gate_terms(hidden, raw_grad):
        left = jnp.sum(hidden * raw_grad, axis=1, keepdims=True)
        terms = jnp.zeros((left.shape[0], 128), f32)
        for i in range(3):
            piece = lax.reduce_precision(left, 8, 7)
            terms = jnp.where(column == 3 * me + i, piece, terms)
            left = left - piece
        return terms.astype(bf16)

    def far_hands(j):
        got = traded(f"rfar_{j}", back[j][half:], (2, 3, 1))
        return [back[j][half : half + CAP]] + [got[m] for m in (1, 2, 3)]

    rest = (grad_gate_pre, grad_up_pre, inputs, raw_grad, hidden, scaled_hidden, parts)
    back = {0: back_of(0, grad_gate_pre, grad_up_pre)}
    back[0], rest = together(back[0], rest)
    hands = far_hands(0)
    back[1] = back_of(1, *rest[:2])
    back[1] = jnp.concatenate([back[1], gate_terms(rest[4], rest[3])], axis=1)
    near_back = jnp.concatenate([back[j][:half] for j in range(steps)], axis=1)
    hands, back, rest, near_back = together(hands, back, rest, near_back)

    def crossing(name, hands):
        far_sum = mm(far_sel, stacked(*hands), ((0,), (0,))).astype(bf16)
        return far_sum

    more = far_hands(1)
    far_sum = crossing(0, hands)
    far_sum, rest, near_back = together(far_sum, rest, near_back)
    crossed = [swap(far_sum, 4)]
    near = traded("rnear", near_back, (2,))
    grad_gw = mm(rest[2], rest[0], ((0,), (0,))).astype(bf16)
    hands, grad_gw, rest, near_back = together(more, grad_gw, rest, near_back)
    far_sum = crossing(1, hands)
    far_sum, rest, near_back = together(far_sum, rest, near_back)
    crossed.append(swap(far_sum, 4))
    near.update(traded("rnear", near_back, (3, 1)))
    grad_uw = mm(rest[2], rest[1], ((0,), (0,))).astype(bf16)
    grad_dw = mm(rest[5], jnp.concatenate(rest[6], axis=1), ((0,), (0,))).astype(bf16)
    total = mm(near_sel, stacked(near_back[:CAP], near[1], near[2], near[3]), ((0,), (0,)))
    total = (total + jnp.concatenate(crossed, axis=1).astype(f32)).astype(bf16)
    terms, grad_input = total[:, width:].astype(f32), total[:, :width]
    wanted = column[None] // 3 == routes[0][:, :, None]
    grad_gates = jnp.sum(jnp.where(wanted, terms[:, None, :], 0.0), axis=2)
    return grad_input[None], grad_gates[None], grad_gw[None], grad_uw[None], grad_dw[None]


def slot_work(codes, scales, cotangent, weights, gate_cols, up_cols, down_rows):
    count, width = codes.shape
    blocks = width // 128
    inputs = (
        (codes.astype(jnp.float32).reshape(count, blocks, 128) * scales[:, :, None])
        .reshape(count, width)
        .astype(jnp.bfloat16)
    )
    gate_pre = jnp.dot(inputs, gate_cols, preferred_element_type=jnp.float32)
    up_pre = jnp.dot(inputs, up_cols, preferred_element_type=jnp.float32)
    sigma = jax.nn.sigmoid(gate_pre)
    swish = gate_pre * sigma
    hidden = swish * up_pre
    scaled_hidden = (weights[:, None] * hidden).astype(jnp.bfloat16)
    grad_down = lax.dot_general(
        scaled_hidden, cotangent, (((0,), (0,)), ((), ())), preferred_element_type=jnp.float32
    )
    raw_grad = lax.dot_general(
        cotangent, down_rows, (((1,), (1,)), ((), ())), preferred_element_type=jnp.float32
    )
    gate_part = jnp.sum(hidden * raw_grad, axis=1)
    grad_hidden = weights[:, None] * raw_grad
    grad_gate_pre = (grad_hidden * up_pre * sigma * (1.0 + gate_pre * (1.0 - sigma))).astype(
        jnp.bfloat16
    )
    grad_up_pre = (grad_hidden * swish).astype(jnp.bfloat16)
    grad_gate_w = lax.dot_general(
        inputs, grad_gate_pre, (((0,), (0,)), ((), ())), preferred_element_type=jnp.float32
    )
    grad_up_w = lax.dot_general(
        inputs, grad_up_pre, (((0,), (0,)), ((), ())), preferred_element_type=jnp.float32
    )
    input_sum = lax.dot_general(
        grad_gate_pre, gate_cols, (((1,), (1,)), ((), ())), preferred_element_type=jnp.float32
    )
    input_sum = input_sum + lax.dot_general(
        grad_up_pre, up_cols, (((1,), (1,)), ((), ())), preferred_element_type=jnp.float32
    )
    return (grad_gate_w, grad_up_w, grad_down, input_sum.astype(jnp.bfloat16), gate_part)


def general(upstream, routes, gates, w_gate, w_up, w_down, stash_q, stash_scale):
    cotangent = shifted(upstream[0], SECTION, -1)
    tok_dev = routes.shape[1]
    topk = routes.shape[2]
    width = cotangent.shape[1]
    groups = lax.axis_size(EXPERT)
    hsplit = groups // EXPERTS
    slots = groups * CAP
    flat = routes[0].reshape(-1)
    onehot = (flat[:, None] == jnp.arange(EXPERTS, dtype=jnp.int32)[None, :]).astype(jnp.int32)
    before = jnp.cumsum(onehot, axis=0) - onehot
    slot = jnp.sum(before * onehot, axis=1)
    target = flat * CAP + slot
    token = jnp.arange(tok_dev * topk, dtype=jnp.int32) // topk
    row_buf = jnp.zeros((EXPERTS * CAP, width), jnp.bfloat16).at[target].set(cotangent[token])
    weight_buf = jnp.zeros((EXPERTS * CAP,), jnp.float32).at[target].set(gates[0].reshape(-1))
    send_rows = jnp.repeat(row_buf.reshape(EXPERTS, CAP, width), hsplit, axis=0)
    send_weights = jnp.repeat(weight_buf.reshape(EXPERTS, CAP), hsplit, axis=0)
    got_rows, got_weights = (
        lax.all_to_all(send_rows, EXPERT, split_axis=0, concat_axis=0, tiled=True),
        lax.all_to_all(
            send_weights.astype(jnp.bfloat16), EXPERT, split_axis=0, concat_axis=0, tiled=True
        ).astype(send_weights.dtype),
    )
    rows = got_rows.reshape(slots, width)
    weights = got_weights.reshape(slots)
    grad_gw, grad_uw, grad_dw, input_part, gate_part = slot_work(
        stash_q[0], stash_scale[0], rows, weights, w_gate[0], w_up[0], w_down[0]
    )
    back_rows, back_gates = (
        lax.all_to_all(
            input_part.reshape(groups, CAP, width), EXPERT, split_axis=0, concat_axis=0, tiled=True
        ),
        lax.all_to_all(
            gate_part.reshape(groups, CAP).astype(jnp.bfloat16),
            EXPERT,
            split_axis=0,
            concat_axis=0,
            tiled=True,
        ).astype(jnp.float32),
    )
    summed = jnp.sum(
        back_rows.reshape(EXPERTS, hsplit, CAP, width).astype(jnp.float32), axis=1
    ).reshape(EXPERTS * CAP, width)
    gate_sum = jnp.sum(
        back_gates.reshape(EXPERTS, hsplit, CAP).astype(jnp.float32), axis=1
    ).reshape(EXPERTS * CAP)
    grad_input = jnp.sum(summed[target].reshape(tok_dev, topk, width), axis=1).astype(jnp.bfloat16)
    grad_gates = gate_sum[target].reshape(tok_dev, topk)
    return (
        grad_input[None],
        grad_gates[None],
        grad_gw.astype(jnp.bfloat16)[None],
        grad_uw.astype(jnp.bfloat16)[None],
        grad_dw.astype(jnp.bfloat16)[None],
    )


def solution(mesh):
    return jax.shard_map(
        relayed if mesh.shape[EXPERT] == EXPERTS else general,
        mesh=mesh,
        in_specs=(
            P(SECTION, EXPERT, None),
            P(SECTION, EXPERT, None),
            P(SECTION, EXPERT, None),
            P(SECTION, None, EXPERT),
            P(SECTION, None, EXPERT),
            P(SECTION, EXPERT, None),
            P(SECTION, EXPERT, None),
            P(SECTION, EXPERT, None),
        ),
        out_specs=(
            P(SECTION, EXPERT, None),
            P(SECTION, EXPERT, None),
            P(SECTION, None, EXPERT),
            P(SECTION, None, EXPERT),
            P(SECTION, EXPERT, None),
        ),
        check_vma=False,
    )
```

```python
import jax
import jax.numpy as jnp
from jax import lax
from jax.experimental import pallas as pl
from jax.experimental.pallas import tpu as pltpu
from jax.sharding import PartitionSpec as P

EXPERT = "expert"
SECTION = "section"
EXPERTS = 8
CAP = 48
OUT_CUTS = (7, 21)
BACK_CUTS = (14, 14)


def shifted(x, axis, by):
    size = lax.axis_size(axis)
    return lax.ppermute(x, axis, [(i, (i + by) % size) for i in range(size)])


def swap(x, bit):
    return lax.ppermute(x, EXPERT, [(i, i ^ bit) for i in range(8)])


def together(*arrays):
    return lax.optimization_barrier(arrays)


def mm(a, b, dims):
    return lax.dot_general(a, b, (dims, ((), ())), preferred_element_type=jnp.float32)


def stacked(*arrays):
    return jnp.concatenate(arrays, axis=0)


def scale_kernel(order, *refs):
    *pairs, out = refs
    for j in range(len(pairs) // 2):
        codes, scales = pairs[2 * j], pairs[2 * j + 1]
        rows = slice(CAP * j, CAP * (j + 1))
        for b in range(codes.shape[1] // 128):
            at = slice(128 * b, 128 * (b + 1))
            got = codes[:, at].astype(jnp.float32) * scales[:, b : b + 1]
            out[rows, at] = got.astype(out.dtype)


def scaled_blocks(order, codes, scales):
    count, width = codes.shape
    at_once = 4
    specs = []
    for j in range(at_once):
        specs.append(pl.BlockSpec((CAP, width), lambda i, order, j=j: (order[at_once * i + j], 0)))
        specs.append(
            pl.BlockSpec((CAP, scales.shape[1]), lambda i, order, j=j: (order[at_once * i + j], 0))
        )
    return pl.pallas_call(
        scale_kernel,
        grid_spec=pltpu.PrefetchScalarGridSpec(
            num_scalar_prefetch=1,
            grid=(count // CAP // at_once,),
            in_specs=specs,
            out_specs=pl.BlockSpec((CAP * at_once, width), lambda i, order: (i, 0)),
        ),
        out_shape=jax.ShapeDtypeStruct((count, width), jnp.bfloat16),
        compiler_params=pltpu.CompilerParams(vmem_limit_bytes=24 * 2**20),
        cost_estimate=pl.CostEstimate(
            flops=1, bytes_accessed=1, transcendentals=0
        ),
    )(order, *[codes, scales] * at_once)


def spans_of(width, cuts):
    blocks, total = width // 128, sum(cuts)
    edges = [128 * (blocks * sum(cuts[:j]) // total) for j in range(len(cuts) + 1)]
    return list(zip(edges[:-1], edges[1:]))


def relayed(upstream, routes, gates, w_gate, w_up, w_down, stash_q, stash_scale):
    bf16, f32 = jnp.bfloat16, jnp.float32
    tokens, width = upstream.shape[1], upstream.shape[2]
    spans, steps = spans_of(width, OUT_CUTS), len(OUT_CUTS)
    half = 4 * CAP
    me = lax.axis_index(EXPERT)
    gate_cols, up_cols, down_rows = w_gate[0], w_up[0], w_down[0]
    codes, scales = stash_q[0], stash_scale[0]
    pieces = [upstream[0, :, lo:hi] for lo, hi in spans]
    xs = [shifted(pieces[0], SECTION, -1)]
    x1 = shifted(pieces[1], SECTION, -1)

    route = routes[0].T
    ids = jnp.arange(EXPERTS, dtype=jnp.int32)
    hit = route[:, None, :] == (ids ^ me)[None, :, None]
    named = jnp.any(hit, axis=0)
    earlier = (jnp.arange(tokens)[:, None] < jnp.arange(tokens)[None, :]).astype(bf16)
    plan = jnp.where(named, mm(named.astype(bf16), earlier, ((1,), (0,))), -1.0)
    gate_of = jnp.sum(jnp.where(hit, gates[0].T[:, None, :], 0.0), axis=0)
    slot_ids = jnp.arange(CAP, dtype=f32)[None, :, None]

    def selection(rows):
        return (rows[:, None, :] == slot_ids).astype(bf16).reshape(-1, tokens)

    def traded(name, rows, which):
        got = {}
        for m in which:
            got[m] = swap(rows[CAP * m : CAP * (m + 1)], m)
        return got

    def pack(sel, rows):
        return mm(sel, rows, ((1,), (0,))).astype(bf16)

    def pieces_of(values):
        got = []
        for _ in range(3):
            got.append(lax.reduce_precision(values, 8, 7))
            values = values - got[-1]
        return jnp.stack(got, axis=-1).astype(bf16)

    def gate_columns(table):
        columns = pieces_of(table).transpose(1, 0, 2).reshape(tokens, -1)
        return jnp.pad(columns, ((0, 0), (0, 128 - columns.shape[1])))

    near_sel = selection(plan[:4])
    both = jnp.stack([plan, gate_of])
    x, pieces, near_sel, both, codes, scales = together(
        xs[0], pieces, near_sel, both, codes, scales
    )

    cross = swap(x, 4)
    own = jnp.concatenate([pack(near_sel, x), pack(near_sel, gate_columns(both[1, :4]))], axis=1)
    own, both, codes = together(own, both, codes)
    near_own = swap(own[2 * CAP :], 2)
    far_both = swap(both, 4)
    inputs = scaled_blocks(me ^ jnp.arange(8, dtype=jnp.int32), codes, scales)
    far_sel = selection(far_both[0, 4:])
    gates_far = pack(far_sel, gate_columns(far_both[1, 4:]))
    cross, x, own, near_own, far_sel, gates_far, inputs = together(
        cross, x1, own, near_own, far_sel, gates_far, inputs
    )

    next_cross = swap(x, 4)
    far = jnp.concatenate([pack(far_sel, cross), gates_far], axis=1)
    far, x, own, near_own, inputs = together(far, x, own, near_own, inputs)
    near_far = swap(far[2 * CAP :], 2)
    own_1 = pack(near_sel, x)
    own_1, own, near_own, inputs = together(own_1, own, near_own, inputs)
    near_own_1 = swap(own_1[2 * CAP :], 2)
    given = swap(stacked(own[CAP : 2 * CAP], near_own[CAP:]), 1)
    gate_pre = mm(inputs, gate_cols, ((1,), (0,)))
    up_pre = mm(inputs, up_cols, ((1,), (0,)))
    near_rows = stacked(own[:CAP], given[:CAP], near_own[:CAP], given[CAP:])
    cross, near_far, near_own_1, near_rows, gate_pre, up_pre, far, own_1 = together(
        next_cross, near_far, near_own_1, near_rows, gate_pre, up_pre, far, own_1
    )

    far_1 = pack(far_sel, cross)
    far_1, far, near_far, own_1, near_own_1, near_rows = together(
        far_1, far, near_far, own_1, near_own_1, near_rows
    )
    got = traded("far_1", far_1, (2, 3, 1))
    given = swap(stacked(far[CAP : 2 * CAP], near_far[CAP:]), 1)
    given_1 = swap(stacked(own_1[CAP : 2 * CAP], near_own_1[CAP:]), 1)
    rows = stacked(near_rows, far[:CAP], given[:CAP], near_far[:CAP], given[CAP:])
    lo = spans[1][0]
    wanted = jnp.arange(128)[None, :] // 3 == jnp.arange(8 * CAP)[:, None] // CAP % 4
    weights = jnp.sum(jnp.where(wanted, rows[:, lo:].astype(f32), 0.0), axis=1, keepdims=True)
    parts = [rows[:, :lo]]
    raw_grad = mm(parts[0], down_rows[:, :lo], ((1,), (1,)))
    sigma = jax.nn.sigmoid(gate_pre)
    swish = gate_pre * sigma
    hidden = swish * up_pre
    scaled_hidden = (weights * hidden).astype(bf16)
    to_gate = weights * up_pre * sigma * (1.0 + gate_pre * (1.0 - sigma))
    to_up = weights * swish
    got, given_1, parts, raw_grad, hidden, scaled_hidden, to_gate, to_up = together(
        got, given_1, parts, raw_grad, hidden, scaled_hidden, to_gate, to_up
    )
    parts.append(
        stacked(
            own_1[:CAP], given_1[:CAP], near_own_1[:CAP], given_1[CAP:], far_1[:CAP], got[1], got[2], got[3]
        )
    )
    raw_grad = raw_grad + mm(parts[1], down_rows[:, lo:], ((1,), (1,)))
    grad_gate_pre = (raw_grad * to_gate).astype(bf16)
    grad_up_pre = (raw_grad * to_up).astype(bf16)

    spans, steps = spans_of(width, BACK_CUTS), len(BACK_CUTS)
    column = jnp.arange(128, dtype=jnp.int32)[None, :]

    def back_of(j, ggp, gup):
        lo, hi = spans[j]
        back = mm(ggp, gate_cols[lo:hi], ((1,), (1,)))
        return (back + mm(gup, up_cols[lo:hi], ((1,), (1,)))).astype(bf16)

    def gate_terms(hidden, raw_grad):
        left = jnp.sum(hidden * raw_grad, axis=1, keepdims=True)
        terms = jnp.zeros((left.shape[0], 128), f32)
        for i in range(3):
            piece = lax.reduce_precision(left, 8, 7)
            terms = jnp.where(column == 3 * me + i, piece, terms)
            left = left - piece
        return terms.astype(bf16)

    def far_hands(j):
        got = traded(f"rfar_{j}", back[j][half:], (2, 3, 1))
        return [back[j][half : half + CAP]] + [got[m] for m in (1, 2, 3)]

    rest = (grad_gate_pre, grad_up_pre, inputs, raw_grad, hidden, scaled_hidden, parts)
    back = {0: back_of(0, grad_gate_pre, grad_up_pre)}
    back[0], rest = together(back[0], rest)
    hands = far_hands(0)
    back[1] = back_of(1, *rest[:2])
    back[1] = jnp.concatenate([back[1], gate_terms(rest[4], rest[3])], axis=1)
    near_back = jnp.concatenate([back[j][:half] for j in range(steps)], axis=1)
    given = swap(stacked(near_back[CAP : 2 * CAP], near_back[3 * CAP :]), 1)
    hands, back, rest, near_back, given = together(hands, back, rest, near_back, given)
    near_sent = stacked(near_back[2 * CAP : 3 * CAP], given[CAP:])

    def crossing(name, hands):
        far_sum = mm(far_sel, stacked(*hands), ((0,), (0,))).astype(bf16)
        return far_sum

    more = far_hands(1)
    far_sum = crossing(0, hands)
    far_sum, rest, near_back = together(far_sum, rest, near_back)
    crossed = [swap(far_sum, 4)]
    near = swap(near_sent, 2)
    grad_gw = mm(rest[2], rest[0], ((0,), (0,))).astype(bf16)
    hands, grad_gw, rest, near_back = together(more, grad_gw, rest, near_back)
    far_sum = crossing(1, hands)
    far_sum, rest, near_back = together(far_sum, rest, near_back)
    crossed.append(swap(far_sum, 4))
    grad_uw = mm(rest[2], rest[1], ((0,), (0,))).astype(bf16)
    grad_dw = mm(rest[5], jnp.concatenate(rest[6], axis=1), ((0,), (0,))).astype(bf16)
    total = mm(near_sel, stacked(near_back[:CAP], given[:CAP], near), ((0,), (0,)))
    total = (total + jnp.concatenate(crossed, axis=1).astype(f32)).astype(bf16)
    terms, grad_input = total[:, width:].astype(f32), total[:, :width]
    wanted = column[None] // 3 == routes[0][:, :, None]
    grad_gates = jnp.sum(jnp.where(wanted, terms[:, None, :], 0.0), axis=2)
    return grad_input[None], grad_gates[None], grad_gw[None], grad_uw[None], grad_dw[None]


def slot_work(codes, scales, cotangent, weights, gate_cols, up_cols, down_rows):
    count, width = codes.shape
    blocks = width // 128
    inputs = (
        (codes.astype(jnp.float32).reshape(count, blocks, 128) * scales[:, :, None])
        .reshape(count, width)
        .astype(jnp.bfloat16)
    )
    gate_pre = jnp.dot(inputs, gate_cols, preferred_element_type=jnp.float32)
    up_pre = jnp.dot(inputs, up_cols, preferred_element_type=jnp.float32)
    sigma = jax.nn.sigmoid(gate_pre)
    swish = gate_pre * sigma
    hidden = swish * up_pre
    scaled_hidden = (weights[:, None] * hidden).astype(jnp.bfloat16)
    grad_down = lax.dot_general(
        scaled_hidden, cotangent, (((0,), (0,)), ((), ())), preferred_element_type=jnp.float32
    )
    raw_grad = lax.dot_general(
        cotangent, down_rows, (((1,), (1,)), ((), ())), preferred_element_type=jnp.float32
    )
    gate_part = jnp.sum(hidden * raw_grad, axis=1)
    grad_hidden = weights[:, None] * raw_grad
    grad_gate_pre = (grad_hidden * up_pre * sigma * (1.0 + gate_pre * (1.0 - sigma))).astype(
        jnp.bfloat16
    )
    grad_up_pre = (grad_hidden * swish).astype(jnp.bfloat16)
    grad_gate_w = lax.dot_general(
        inputs, grad_gate_pre, (((0,), (0,)), ((), ())), preferred_element_type=jnp.float32
    )
    grad_up_w = lax.dot_general(
        inputs, grad_up_pre, (((0,), (0,)), ((), ())), preferred_element_type=jnp.float32
    )
    input_sum = lax.dot_general(
        grad_gate_pre, gate_cols, (((1,), (1,)), ((), ())), preferred_element_type=jnp.float32
    )
    input_sum = input_sum + lax.dot_general(
        grad_up_pre, up_cols, (((1,), (1,)), ((), ())), preferred_element_type=jnp.float32
    )
    return (grad_gate_w, grad_up_w, grad_down, input_sum.astype(jnp.bfloat16), gate_part)


def general(upstream, routes, gates, w_gate, w_up, w_down, stash_q, stash_scale):
    cotangent = shifted(upstream[0], SECTION, -1)
    tok_dev = routes.shape[1]
    topk = routes.shape[2]
    width = cotangent.shape[1]
    groups = lax.axis_size(EXPERT)
    hsplit = groups // EXPERTS
    slots = groups * CAP
    flat = routes[0].reshape(-1)
    onehot = (flat[:, None] == jnp.arange(EXPERTS, dtype=jnp.int32)[None, :]).astype(jnp.int32)
    before = jnp.cumsum(onehot, axis=0) - onehot
    slot = jnp.sum(before * onehot, axis=1)
    target = flat * CAP + slot
    token = jnp.arange(tok_dev * topk, dtype=jnp.int32) // topk
    row_buf = jnp.zeros((EXPERTS * CAP, width), jnp.bfloat16).at[target].set(cotangent[token])
    weight_buf = jnp.zeros((EXPERTS * CAP,), jnp.float32).at[target].set(gates[0].reshape(-1))
    send_rows = jnp.repeat(row_buf.reshape(EXPERTS, CAP, width), hsplit, axis=0)
    send_weights = jnp.repeat(weight_buf.reshape(EXPERTS, CAP), hsplit, axis=0)
    got_rows, got_weights = (
        lax.all_to_all(send_rows, EXPERT, split_axis=0, concat_axis=0, tiled=True),
        lax.all_to_all(
            send_weights.astype(jnp.bfloat16), EXPERT, split_axis=0, concat_axis=0, tiled=True
        ).astype(send_weights.dtype),
    )
    rows = got_rows.reshape(slots, width)
    weights = got_weights.reshape(slots)
    grad_gw, grad_uw, grad_dw, input_part, gate_part = slot_work(
        stash_q[0], stash_scale[0], rows, weights, w_gate[0], w_up[0], w_down[0]
    )
    back_rows, back_gates = (
        lax.all_to_all(
            input_part.reshape(groups, CAP, width), EXPERT, split_axis=0, concat_axis=0, tiled=True
        ),
        lax.all_to_all(
            gate_part.reshape(groups, CAP).astype(jnp.bfloat16),
            EXPERT,
            split_axis=0,
            concat_axis=0,
            tiled=True,
        ).astype(jnp.float32),
    )
    summed = jnp.sum(
        back_rows.reshape(EXPERTS, hsplit, CAP, width).astype(jnp.float32), axis=1
    ).reshape(EXPERTS * CAP, width)
    gate_sum = jnp.sum(
        back_gates.reshape(EXPERTS, hsplit, CAP).astype(jnp.float32), axis=1
    ).reshape(EXPERTS * CAP)
    grad_input = jnp.sum(summed[target].reshape(tok_dev, topk, width), axis=1).astype(jnp.bfloat16)
    grad_gates = gate_sum[target].reshape(tok_dev, topk)
    return (
        grad_input[None],
        grad_gates[None],
        grad_gw.astype(jnp.bfloat16)[None],
        grad_uw.astype(jnp.bfloat16)[None],
        grad_dw.astype(jnp.bfloat16)[None],
    )


def solution(mesh):
    return jax.shard_map(
        relayed if mesh.shape[EXPERT] == EXPERTS else general,
        mesh=mesh,
        in_specs=(
            P(SECTION, EXPERT, None),
            P(SECTION, EXPERT, None),
            P(SECTION, EXPERT, None),
            P(SECTION, None, EXPERT),
            P(SECTION, None, EXPERT),
            P(SECTION, EXPERT, None),
            P(SECTION, EXPERT, None),
            P(SECTION, EXPERT, None),
        ),
        out_specs=(
            P(SECTION, EXPERT, None),
            P(SECTION, EXPERT, None),
            P(SECTION, None, EXPERT),
            P(SECTION, None, EXPERT),
            P(SECTION, EXPERT, None),
        ),
        check_vma=False,
    )
```

```python
import jax
import jax.numpy as jnp
from jax import lax
from jax.experimental import pallas as pl
from jax.experimental.pallas import tpu as pltpu
from jax.sharding import PartitionSpec as P

EXPERT = "expert"
SECTION = "section"
EXPERTS = 8
CAP = 48
OUT_CUTS = (7, 21)
BACK_CUTS = (14, 14)


def shifted(x, axis, by):
    size = lax.axis_size(axis)
    return lax.ppermute(x, axis, [(i, (i + by) % size) for i in range(size)])


def swap(x, bit):
    return lax.ppermute(x, EXPERT, [(i, i ^ bit) for i in range(8)])


def together(*arrays):
    return lax.optimization_barrier(arrays)


def mm(a, b, dims):
    return lax.dot_general(a, b, (dims, ((), ())), preferred_element_type=jnp.float32)


def stacked(*arrays):
    return jnp.concatenate(arrays, axis=0)


def scale_kernel(order, *refs):
    *pairs, out = refs
    for j in range(len(pairs) // 2):
        codes, scales = pairs[2 * j], pairs[2 * j + 1]
        rows = slice(CAP * j, CAP * (j + 1))
        for b in range(codes.shape[1] // 128):
            at = slice(128 * b, 128 * (b + 1))
            got = codes[:, at].astype(jnp.float32) * scales[:, b : b + 1]
            out[rows, at] = got.astype(out.dtype)


def scaled_blocks(order, codes, scales):
    count, width = codes.shape
    at_once = 4
    specs = []
    for j in range(at_once):
        specs.append(pl.BlockSpec((CAP, width), lambda i, order, j=j: (order[at_once * i + j], 0)))
        specs.append(
            pl.BlockSpec((CAP, scales.shape[1]), lambda i, order, j=j: (order[at_once * i + j], 0))
        )
    return pl.pallas_call(
        scale_kernel,
        grid_spec=pltpu.PrefetchScalarGridSpec(
            num_scalar_prefetch=1,
            grid=(count // CAP // at_once,),
            in_specs=specs,
            out_specs=pl.BlockSpec((CAP * at_once, width), lambda i, order: (i, 0)),
        ),
        out_shape=jax.ShapeDtypeStruct((count, width), jnp.bfloat16),
        compiler_params=pltpu.CompilerParams(vmem_limit_bytes=24 * 2**20),
        cost_estimate=pl.CostEstimate(
            flops=1, bytes_accessed=1, transcendentals=0
        ),
    )(order, *[codes, scales] * at_once)


def spans_of(width, cuts):
    blocks, total = width // 128, sum(cuts)
    edges = [128 * (blocks * sum(cuts[:j]) // total) for j in range(len(cuts) + 1)]
    return list(zip(edges[:-1], edges[1:]))


def relayed(upstream, routes, gates, w_gate, w_up, w_down, stash_q, stash_scale):
    bf16, f32 = jnp.bfloat16, jnp.float32
    tokens, width = upstream.shape[1], upstream.shape[2]
    spans, steps = spans_of(width, OUT_CUTS), len(OUT_CUTS)
    half = 4 * CAP
    me = lax.axis_index(EXPERT)
    gate_cols, up_cols, down_rows = w_gate[0], w_up[0], w_down[0]
    codes, scales = stash_q[0], stash_scale[0]
    pieces = [upstream[0, :, lo:hi] for lo, hi in spans]
    xs = [shifted(pieces[0], SECTION, -1)]
    x1 = shifted(pieces[1], SECTION, -1)

    route = routes[0].T
    ids = jnp.arange(EXPERTS, dtype=jnp.int32)
    hit = route[:, None, :] == (ids ^ me)[None, :, None]
    named = jnp.any(hit, axis=0)
    earlier = (jnp.arange(tokens)[:, None] < jnp.arange(tokens)[None, :]).astype(bf16)
    plan = jnp.where(named, mm(named.astype(bf16), earlier, ((1,), (0,))), -1.0)
    gate_of = jnp.sum(jnp.where(hit, gates[0].T[:, None, :], 0.0), axis=0)
    slot_ids = jnp.arange(CAP, dtype=f32)[None, :, None]

    def selection(rows):
        return (rows[:, None, :] == slot_ids).astype(bf16).reshape(-1, tokens)

    def traded(name, rows, which):
        got = {}
        for m in which:
            got[m] = swap(rows[CAP * m : CAP * (m + 1)], m)
        return got

    def pack(sel, rows):
        return mm(sel, rows, ((1,), (0,))).astype(bf16)

    def pieces_of(values):
        got = []
        for _ in range(3):
            got.append(lax.reduce_precision(values, 8, 7))
            values = values - got[-1]
        return jnp.stack(got, axis=-1).astype(bf16)

    def gate_columns(table):
        columns = pieces_of(table).transpose(1, 0, 2).reshape(tokens, -1)
        return jnp.pad(columns, ((0, 0), (0, 128 - columns.shape[1])))

    near_sel = selection(plan[:4])
    both = jnp.stack([plan, gate_of])
    x, pieces, near_sel, both, codes, scales = together(
        xs[0], pieces, near_sel, both, codes, scales
    )

    cross = swap(x, 4)
    own = jnp.concatenate([pack(near_sel, x), pack(near_sel, gate_columns(both[1, :4]))], axis=1)
    own, both, codes = together(own, both, codes)
    near_own = swap(own[2 * CAP :], 2)
    far_both = swap(both, 4)
    inputs = scaled_blocks(me ^ jnp.arange(8, dtype=jnp.int32), codes, scales)
    far_sel = selection(far_both[0, 4:])
    gates_far = pack(far_sel, gate_columns(far_both[1, 4:]))
    cross, x, own, near_own, far_sel, gates_far, inputs = together(
        cross, x1, own, near_own, far_sel, gates_far, inputs
    )

    next_cross = swap(x, 4)
    far = jnp.concatenate([pack(far_sel, cross), gates_far], axis=1)
    far, x, own, near_own, inputs = together(far, x, own, near_own, inputs)
    near_far = swap(far[2 * CAP :], 2)
    own_1 = pack(near_sel, x)
    own_1, own, near_own, inputs = together(own_1, own, near_own, inputs)
    near_own_1 = swap(own_1[2 * CAP :], 2)
    given = swap(stacked(own[CAP : 2 * CAP], near_own[CAP:]), 1)
    gate_pre = mm(inputs, gate_cols, ((1,), (0,)))
    up_pre = mm(inputs, up_cols, ((1,), (0,)))
    near_rows = stacked(own[:CAP], given[:CAP], near_own[:CAP], given[CAP:])
    cross, near_far, near_own_1, near_rows, gate_pre, up_pre, far, own_1 = together(
        next_cross, near_far, near_own_1, near_rows, gate_pre, up_pre, far, own_1
    )

    far_1 = pack(far_sel, cross)
    far_1, far, near_far, own_1, near_own_1, near_rows = together(
        far_1, far, near_far, own_1, near_own_1, near_rows
    )
    got = traded("far_1", far_1, (2, 3, 1))
    given = swap(stacked(far[CAP : 2 * CAP], near_far[CAP:]), 1)
    given_1 = swap(stacked(own_1[CAP : 2 * CAP], near_own_1[CAP:]), 1)
    rows = stacked(near_rows, far[:CAP], given[:CAP], near_far[:CAP], given[CAP:])
    lo = spans[1][0]
    wanted = jnp.arange(128)[None, :] // 3 == jnp.arange(8 * CAP)[:, None] // CAP % 4
    weights = jnp.sum(jnp.where(wanted, rows[:, lo:].astype(f32), 0.0), axis=1, keepdims=True)
    parts = [rows[:, :lo]]
    raw_grad = mm(parts[0], down_rows[:, :lo], ((1,), (1,)))
    sigma = jax.nn.sigmoid(gate_pre)
    swish = gate_pre * sigma
    hidden = swish * up_pre
    scaled_hidden = (weights * hidden).astype(bf16)
    to_gate = weights * up_pre * sigma * (1.0 + gate_pre * (1.0 - sigma))
    to_up = weights * swish
    got, given_1, parts, raw_grad, hidden, scaled_hidden, to_gate, to_up = together(
        got, given_1, parts, raw_grad, hidden, scaled_hidden, to_gate, to_up
    )
    parts.append(
        stacked(
            own_1[:CAP], given_1[:CAP], near_own_1[:CAP], given_1[CAP:], far_1[:CAP], got[1], got[2], got[3]
        )
    )
    raw_grad = raw_grad + mm(parts[1], down_rows[:, lo:], ((1,), (1,)))
    grad_gate_pre = (raw_grad * to_gate).astype(bf16)
    grad_up_pre = (raw_grad * to_up).astype(bf16)

    spans, steps = spans_of(width, BACK_CUTS), len(BACK_CUTS)
    column = jnp.arange(128, dtype=jnp.int32)[None, :]

    def back_of(j, ggp, gup):
        lo, hi = spans[j]
        back = mm(ggp, gate_cols[lo:hi], ((1,), (1,)))
        return (back + mm(gup, up_cols[lo:hi], ((1,), (1,)))).astype(bf16)

    def gate_terms(hidden, raw_grad):
        left = jnp.sum(hidden * raw_grad, axis=1, keepdims=True)
        terms = jnp.zeros((left.shape[0], 128), f32)
        for i in range(3):
            piece = lax.reduce_precision(left, 8, 7)
            terms = jnp.where(column == 3 * me + i, piece, terms)
            left = left - piece
        return terms.astype(bf16)

    def far_hands(j):
        got = traded(f"rfar_{j}", back[j][half:], (2, 3, 1))
        return [back[j][half : half + CAP]] + [got[m] for m in (1, 2, 3)]

    rest = (grad_gate_pre, grad_up_pre, inputs, raw_grad, hidden, scaled_hidden, parts)
    back = {0: back_of(0, grad_gate_pre, grad_up_pre)}
    back[0], rest = together(back[0], rest)
    hands = far_hands(0)
    back[1] = back_of(1, *rest[:2])
    back[1] = jnp.concatenate([back[1], gate_terms(rest[4], rest[3])], axis=1)
    near_back = jnp.concatenate([back[j][:half] for j in range(steps)], axis=1)
    given = swap(stacked(near_back[CAP : 2 * CAP], near_back[3 * CAP :]), 1)
    far_back = back[1][half:]
    far_given = swap(stacked(far_back[CAP : 2 * CAP], far_back[3 * CAP :]), 1)
    hands, back, rest, near_back, given, far_given = together(
        hands, back, rest, near_back, given, far_given
    )
    far_back = back[1][half:]
    near_sent = stacked(near_back[2 * CAP : 3 * CAP], given[CAP:])

    def crossing(name, hands):
        far_sum = mm(far_sel, stacked(*hands), ((0,), (0,))).astype(bf16)
        return far_sum

    far_got = swap(stacked(far_back[2 * CAP : 3 * CAP], far_given[CAP:]), 2)
    more = [far_back[:CAP], far_given[:CAP], far_got[:CAP], far_got[CAP:]]
    far_sum = crossing(0, hands)
    far_sum, rest, near_back = together(far_sum, rest, near_back)
    crossed = [swap(far_sum, 4)]
    near = swap(near_sent, 2)
    grad_gw = mm(rest[2], rest[0], ((0,), (0,))).astype(bf16)
    hands, grad_gw, rest, near_back = together(more, grad_gw, rest, near_back)
    far_sum = crossing(1, hands)
    far_sum, rest, near_back = together(far_sum, rest, near_back)
    crossed.append(swap(far_sum, 4))
    grad_uw = mm(rest[2], rest[1], ((0,), (0,))).astype(bf16)
    grad_dw = mm(rest[5], jnp.concatenate(rest[6], axis=1), ((0,), (0,))).astype(bf16)
    total = mm(near_sel, stacked(near_back[:CAP], given[:CAP], near), ((0,), (0,)))
    total = (total + jnp.concatenate(crossed, axis=1).astype(f32)).astype(bf16)
    terms, grad_input = total[:, width:].astype(f32), total[:, :width]
    wanted = column[None] // 3 == routes[0][:, :, None]
    grad_gates = jnp.sum(jnp.where(wanted, terms[:, None, :], 0.0), axis=2)
    return grad_input[None], grad_gates[None], grad_gw[None], grad_uw[None], grad_dw[None]


def slot_work(codes, scales, cotangent, weights, gate_cols, up_cols, down_rows):
    count, width = codes.shape
    blocks = width // 128
    inputs = (
        (codes.astype(jnp.float32).reshape(count, blocks, 128) * scales[:, :, None])
        .reshape(count, width)
        .astype(jnp.bfloat16)
    )
    gate_pre = jnp.dot(inputs, gate_cols, preferred_element_type=jnp.float32)
    up_pre = jnp.dot(inputs, up_cols, preferred_element_type=jnp.float32)
    sigma = jax.nn.sigmoid(gate_pre)
    swish = gate_pre * sigma
    hidden = swish * up_pre
    scaled_hidden = (weights[:, None] * hidden).astype(jnp.bfloat16)
    grad_down = lax.dot_general(
        scaled_hidden, cotangent, (((0,), (0,)), ((), ())), preferred_element_type=jnp.float32
    )
    raw_grad = lax.dot_general(
        cotangent, down_rows, (((1,), (1,)), ((), ())), preferred_element_type=jnp.float32
    )
    gate_part = jnp.sum(hidden * raw_grad, axis=1)
    grad_hidden = weights[:, None] * raw_grad
    grad_gate_pre = (grad_hidden * up_pre * sigma * (1.0 + gate_pre * (1.0 - sigma))).astype(
        jnp.bfloat16
    )
    grad_up_pre = (grad_hidden * swish).astype(jnp.bfloat16)
    grad_gate_w = lax.dot_general(
        inputs, grad_gate_pre, (((0,), (0,)), ((), ())), preferred_element_type=jnp.float32
    )
    grad_up_w = lax.dot_general(
        inputs, grad_up_pre, (((0,), (0,)), ((), ())), preferred_element_type=jnp.float32
    )
    input_sum = lax.dot_general(
        grad_gate_pre, gate_cols, (((1,), (1,)), ((), ())), preferred_element_type=jnp.float32
    )
    input_sum = input_sum + lax.dot_general(
        grad_up_pre, up_cols, (((1,), (1,)), ((), ())), preferred_element_type=jnp.float32
    )
    return (grad_gate_w, grad_up_w, grad_down, input_sum.astype(jnp.bfloat16), gate_part)


def general(upstream, routes, gates, w_gate, w_up, w_down, stash_q, stash_scale):
    cotangent = shifted(upstream[0], SECTION, -1)
    tok_dev = routes.shape[1]
    topk = routes.shape[2]
    width = cotangent.shape[1]
    groups = lax.axis_size(EXPERT)
    hsplit = groups // EXPERTS
    slots = groups * CAP
    flat = routes[0].reshape(-1)
    onehot = (flat[:, None] == jnp.arange(EXPERTS, dtype=jnp.int32)[None, :]).astype(jnp.int32)
    before = jnp.cumsum(onehot, axis=0) - onehot
    slot = jnp.sum(before * onehot, axis=1)
    target = flat * CAP + slot
    token = jnp.arange(tok_dev * topk, dtype=jnp.int32) // topk
    row_buf = jnp.zeros((EXPERTS * CAP, width), jnp.bfloat16).at[target].set(cotangent[token])
    weight_buf = jnp.zeros((EXPERTS * CAP,), jnp.float32).at[target].set(gates[0].reshape(-1))
    send_rows = jnp.repeat(row_buf.reshape(EXPERTS, CAP, width), hsplit, axis=0)
    send_weights = jnp.repeat(weight_buf.reshape(EXPERTS, CAP), hsplit, axis=0)
    got_rows, got_weights = (
        lax.all_to_all(send_rows, EXPERT, split_axis=0, concat_axis=0, tiled=True),
        lax.all_to_all(
            send_weights.astype(jnp.bfloat16), EXPERT, split_axis=0, concat_axis=0, tiled=True
        ).astype(send_weights.dtype),
    )
    rows = got_rows.reshape(slots, width)
    weights = got_weights.reshape(slots)
    grad_gw, grad_uw, grad_dw, input_part, gate_part = slot_work(
        stash_q[0], stash_scale[0], rows, weights, w_gate[0], w_up[0], w_down[0]
    )
    back_rows, back_gates = (
        lax.all_to_all(
            input_part.reshape(groups, CAP, width), EXPERT, split_axis=0, concat_axis=0, tiled=True
        ),
        lax.all_to_all(
            gate_part.reshape(groups, CAP).astype(jnp.bfloat16),
            EXPERT,
            split_axis=0,
            concat_axis=0,
            tiled=True,
        ).astype(jnp.float32),
    )
    summed = jnp.sum(
        back_rows.reshape(EXPERTS, hsplit, CAP, width).astype(jnp.float32), axis=1
    ).reshape(EXPERTS * CAP, width)
    gate_sum = jnp.sum(
        back_gates.reshape(EXPERTS, hsplit, CAP).astype(jnp.float32), axis=1
    ).reshape(EXPERTS * CAP)
    grad_input = jnp.sum(summed[target].reshape(tok_dev, topk, width), axis=1).astype(jnp.bfloat16)
    grad_gates = gate_sum[target].reshape(tok_dev, topk)
    return (
        grad_input[None],
        grad_gates[None],
        grad_gw.astype(jnp.bfloat16)[None],
        grad_uw.astype(jnp.bfloat16)[None],
        grad_dw.astype(jnp.bfloat16)[None],
    )


def solution(mesh):
    return jax.shard_map(
        relayed if mesh.shape[EXPERT] == EXPERTS else general,
        mesh=mesh,
        in_specs=(
            P(SECTION, EXPERT, None),
            P(SECTION, EXPERT, None),
            P(SECTION, EXPERT, None),
            P(SECTION, None, EXPERT),
            P(SECTION, None, EXPERT),
            P(SECTION, EXPERT, None),
            P(SECTION, EXPERT, None),
            P(SECTION, EXPERT, None),
        ),
        out_specs=(
            P(SECTION, EXPERT, None),
            P(SECTION, EXPERT, None),
            P(SECTION, None, EXPERT),
            P(SECTION, None, EXPERT),
            P(SECTION, EXPERT, None),
        ),
        check_vma=False,
    )
```
